256 devices in a mesh: row: 64 (over y, z_lo, x, core), col: 4 (over z_hi).
Axes of the slice: x: 4, y: 4, z: 8 (z_hi: 4, z_lo: 2; z = z_hi * 2 + z_lo), core: 2. Of those that a mesh axis runs over, the one named last changes fastest.
Arguments:
- tokens: bfloat16 [1536, 128, 128], P('row', 'col'), may hold values from -6 to 6
- attn_gain: float32 [2, 128], replicated, may hold values from 0.1 to 1.9
- w_qkv: bfloat16 [2, 128, 384], replicated, may hold values from -0.5 to 0.5
- score_scale: float32 [2, 2], replicated, may hold values from 2 to 10
- w_out: bfloat16 [2, 128, 128], replicated, may hold values from -0.5 to 0.5
- mlp_gain: float32 [2, 128], replicated, may hold values from 0.1 to 1.9
- w_in: bfloat16 [2, 128, 768], replicated, may hold values from -0.5 to 0.5
- down_weight: bfloat16 [2, 384, 128], replicated, may hold values from -0.3125 to 0.3125
Outputs:
- result: bfloat16 [1536, 128, 128], P('row', 'col')
The draws below stay inside these ranges and needn't reach their ends.
All inputs are finite; a program needn't handle non-finite values.
Results may differ from the reference program's by a relative error of at most 0.025.
Values may be sent and summed in bfloat16 or wider, within the bound.
A program may use at most 128 MiB of HBM per device.

```python
import math
import jax
import jax.numpy as jnp
from jax import lax

D = 128
HEADS = 2
FF = 384
WIN = 7
SECOND_DILATION = 8
LAYERS = 2
ROWS_DEV = 24
HEIGHT = 1536
WIDTH = 128
N_ROW = 64


def block_scale(key, dims, split, low, top_value):
    level, own = 1.0, jax.random.fold_in(key, 6)
    for axis_at, parts in split:
        draws = jnp.exp(jax.random.uniform(jax.random.fold_in(own, axis_at), (parts,), jnp.float32, low / len(split), top_value / len(split)))
        level = level * jnp.repeat(draws, dims[axis_at] // parts).reshape([-1 if axis == axis_at else 1 for axis in range(len(dims))])
    return level


def normal_values(key, dims, deviation, bound, split=(), kind=jnp.bfloat16):
    level = block_scale(key, dims, split, -0.22, 0.18) if split else 1.0
    drawn = jax.random.normal(key, dims, jnp.float32) * deviation * level
    return jnp.minimum(jnp.maximum(drawn, -bound), bound).astype(kind)


def setup_inputs(seed: int = 0) -> dict:
    key_list = jax.random.split(jax.random.key(seed), 9)
    return {
        "tokens": normal_values(key_list[0], (HEIGHT, WIDTH, D), 1.0, 6.0, ((0, 64), (1, 4))),
        "attn_gain": jnp.clip(1.0 + 0.18 * jax.random.normal(key_list[1], (LAYERS, D), jnp.float32), 0.1, 1.9),
        "w_qkv": normal_values(key_list[2], (LAYERS, D, 3 * D), D ** -0.5, 0.5),
        "score_scale": jnp.clip(jnp.exp(jax.random.uniform(key_list[3], (LAYERS, HEADS), jnp.float32, math.log(2.0), math.log(10.0))), 2.0, 10.0),
        "w_out": normal_values(key_list[4], (LAYERS, D, D), D ** -0.5, 0.5),
        "mlp_gain": jnp.clip(1.0 + 0.18 * jax.random.normal(key_list[5], (LAYERS, D), jnp.float32), 0.1, 1.9),
        "w_in": normal_values(key_list[6], (LAYERS, D, 2 * FF), D ** -0.5, 0.5),
        "down_weight": normal_values(key_list[7], (LAYERS, FF, D), FF ** -0.5, 0.3125),
    }


def norm_rows(values, gain):
    floats = values.astype(jnp.float32)
    scale = lax.rsqrt(lax.optimization_barrier(jnp.mean(floats * floats, axis=-1, keepdims=True)) + 1e-06)
    return (floats * scale * gain).astype(jnp.bfloat16)

def project_rows(normed, weight):
    rows, cols, width = normed.shape
    product = jnp.dot(normed.reshape(rows * cols, width), weight, preferred_element_type=jnp.float32)
    return product.astype(jnp.bfloat16).reshape(rows, cols, weight.shape[1])

def local_window_attend(query, keyval, valid, scale, dilation_step, window, heads):
    rows, cols, width = query.shape
    size = width // heads
    query_f = query.astype(jnp.float32).reshape(rows, cols, heads, size)
    query_unit = query_f * lax.rsqrt(lax.optimization_barrier(jnp.sum(query_f * query_f, axis=-1, keepdims=True)) + 1e-06) * scale[:, None]
    big_rows, big_cols = (keyval.shape[0], keyval.shape[1])
    keys = keyval[:, :, :width].reshape(big_rows, big_cols, heads, size)
    vals = keyval[:, :, width:].reshape(big_rows, big_cols, heads, size)
    keys_f = keys.astype(jnp.float32)
    key_inv = lax.rsqrt(lax.optimization_barrier(jnp.sum(keys_f * keys_f, axis=-1)) + 1e-06)
    numer = jnp.zeros((rows, cols, heads, size), jnp.float32)
    denom = jnp.zeros((rows, cols, heads), jnp.float32)
    for step_a in range(window):
        for step_b in range(window):
            top = step_a * dilation_step
            left = step_b * dilation_step
            key_part = keys[top:top + rows, left:left + cols].astype(jnp.float32)
            score = lax.optimization_barrier(jnp.sum(query_unit * key_part, axis=-1)) * key_inv[top:top + rows, left:left + cols]
            weight = jnp.exp(score) * valid[top:top + rows, left:left + cols, None]
            denom = denom + weight
            numer = numer + weight[..., None] * vals[top:top + rows, left:left + cols].astype(jnp.float32)
    attended = numer / denom[..., None]
    return attended.reshape(rows, cols, width).astype(jnp.bfloat16)

def finish_layer(values, attended, w_out, mlp_gain, w_in, down_weight):
    rows, cols, width = values.shape
    hidden_ff = down_weight.shape[0]
    proj = jnp.dot(attended.reshape(rows * cols, width), w_out, preferred_element_type=jnp.float32)
    first = (values.astype(jnp.float32) + proj.reshape(rows, cols, width)).astype(jnp.bfloat16)
    normed = norm_rows(first, mlp_gain)
    inner = jnp.dot(normed.reshape(rows * cols, width), w_in, preferred_element_type=jnp.float32)
    hidden = (inner[:, :hidden_ff] * jax.nn.gelu(inner[:, hidden_ff:], approximate=True)).astype(jnp.bfloat16)
    down = jnp.dot(hidden, down_weight, preferred_element_type=jnp.float32).reshape(rows, cols, width)
    return (first.astype(jnp.float32) + down).astype(jnp.bfloat16)

def reference(tokens, attn_gain, w_qkv, score_scale, w_out, mlp_gain, w_in, down_weight):
    values = tokens
    for layer_index in range(LAYERS):
        dilation_step = 1 if layer_index == 0 else SECOND_DILATION
        reach = WIN // 2 * dilation_step
        normed = norm_rows(values, attn_gain[layer_index])
        padded = jnp.pad(normed, ((reach, reach), (reach, reach), (0, 0)))
        col_ids = jnp.arange(WIDTH + 2 * reach, dtype=jnp.int32) - reach
        col_ok = (col_ids >= 0) & (col_ids < WIDTH)

        def band(index):
            start = (index * ROWS_DEV).astype(jnp.int32)
            window_rows = lax.dynamic_slice_in_dim(padded, start, ROWS_DEV + 2 * reach, 0)
            own = lax.dynamic_slice_in_dim(values, start, ROWS_DEV, 0)
            centre = window_rows[reach:reach + ROWS_DEV, reach:reach + WIDTH]
            query = project_rows(centre, w_qkv[layer_index][:, :D])
            keyval = project_rows(window_rows, w_qkv[layer_index][:, D:])
            row_ids = start - reach + jnp.arange(ROWS_DEV + 2 * reach, dtype=jnp.int32)
            row_inside = (row_ids >= 0) & (row_ids < HEIGHT)
            valid = (row_inside[:, None] & col_ok[None, :]).astype(jnp.float32)
            attended = local_window_attend(query, keyval, valid, score_scale[layer_index], dilation_step, WIN, HEADS)
            return finish_layer(own, attended, w_out[layer_index], mlp_gain[layer_index], w_in[layer_index], down_weight[layer_index])
        bands = lax.map(band, jnp.arange(N_ROW, dtype=jnp.int32))
        values = bands.reshape(HEIGHT, WIDTH, D)
    return values
```

```python
import functools

import jax
import jax.numpy as jnp
import numpy as np
from jax import lax
from jax.experimental import pallas as pl
from jax.experimental.pallas import tpu as pltpu
from jax.sharding import PartitionSpec as P

F32, BF16 = jnp.float32, jnp.bfloat16
MESH = pl.DeviceIdType.MESH
D = 128
FF = 384
ROWS, COLS = 24, 32
STEP = 8
TRIPS = ROWS // STEP
WIDE = 24
CHUNKS = 4
PER = STEP // CHUNKS
TOK = PER * TRIPS * COLS
SIDE = PER * TRIPS * WIDE
BLOCK = TRIPS * (COLS + 2 * WIDE)
LOG2E = 1.4426950408889634


def near_masks():
    a = np.arange(2)[:, None, None, None]
    c = np.arange(COLS)[None, :, None, None]
    kr = np.arange(8)[None, None, :, None]
    rows = (kr - a >= 0) & (kr - a <= 6)
    own = rows & (abs(np.arange(COLS) - c) <= 3)
    slot = np.arange(8)
    side = rows & (abs(np.where(slot < 4, COLS + slot, slot - 8) - c) <= 3)
    return own.reshape(64, 256), side.reshape(64, 64)


def far_mask():
    t = np.arange(TRIPS)[:, None, None]
    c = np.arange(COLS)[None, :, None]
    key_row, key_col = [], []
    for d in range(3):
        for cols in (np.arange(COLS), np.arange(WIDE) - WIDE, np.arange(WIDE) + COLS):
            for t2 in range(TRIPS):
                key_row += [TRIPS * (d - 1) + t2] * len(cols)
                key_col += list(cols)
    key_row, key_col = np.array(key_row), np.array(key_col)
    ok = (abs(key_row - t) <= 3) & ((key_col - c) % STEP == 0) & (abs(key_col - c) <= 3 * STEP)
    return ok.reshape(TRIPS * COLS, 3 * BLOCK)


def dot(a, b):
    return jnp.dot(a, b, preferred_element_type=F32)


def dot_nt(a, b):
    return lax.dot_general(a, b, (((1,), (1,)), ((), ())), preferred_element_type=F32)


def norm(x, gain):
    return x * lax.rsqrt(jnp.mean(x * x, axis=-1, keepdims=True) + 1e-6) * gain


def unit(x, ones):
    return x * lax.rsqrt(dot((x * x).astype(BF16), ones) + 1e-6)


def kernel(
    tok, again, wqkv, sscale, wout, mgain, win, wdown, mown, mside, mfar, out,
    k0, v0, k0s, v0s, q0, x2, upx, dnx, pack_l, pack_r, col_l, col_r,
    h1, hl, hr, rc, lr, k1, v1, s_near, r_near, s_far, r_far,
):
    row, col = lax.axis_index("row"), lax.axis_index("col")
    n_row, n_col = lax.axis_size("row"), lax.axis_size("col")
    up, down = lax.rem(row + n_row - 1, n_row), lax.rem(row + 1, n_row)
    left, right = lax.rem(col + n_col - 1, n_col), lax.rem(col + 1, n_col)

    barrier = pltpu.get_barrier_semaphore()
    around = [
        (down, col), (up, col), (row, right), (row, left),
        (down, right), (up, right), (down, left), (up, left),
    ]
    for device in around:
        pl.semaphore_signal(barrier, inc=1, device_id=device, device_id_type=MESH)

    has_up = (row > 0).astype(F32)
    has_down = (row < n_row - 1).astype(F32)
    has_left = (col > 0).astype(F32)
    has_right = (col < n_col - 1).astype(F32)
    row_ok = (has_up, jnp.float32(1), has_down)

    x0 = tok[...].astype(F32)
    pack_l[...] = x0[:, :8].reshape(ROWS * 8, D).astype(BF16)
    pack_r[...] = x0[:, COLS - 8 :].reshape(ROWS * 8, D).astype(BF16)

    pl.semaphore_wait(barrier, 8)

    def send(src, dst, sems, at, device):
        copy = pltpu.make_async_remote_copy(
            src_ref=src, dst_ref=dst, send_sem=sems[0].at[at], recv_sem=sems[1].at[at],
            device_id=device, device_id_type=MESH,
        )
        copy.start()
        return copy

    edge = ROWS * 8
    near = [
        (pack_r, col_l.at[pl.ds(32, edge)]),
        (pack_l, col_r.at[pl.ds(32, edge)]),
        (tok.at[pl.ds(ROWS - 3, 3)], upx),
        (tok.at[pl.ds(0, 3)], dnx),
        (pack_r.at[pl.ds(edge - 32, 32)], col_l.at[pl.ds(0, 32)]),
        (pack_r.at[pl.ds(0, 32)], col_l.at[pl.ds(edge + 32, 32)]),
        (pack_l.at[pl.ds(edge - 32, 32)], col_r.at[pl.ds(0, 32)]),
        (pack_l.at[pl.ds(0, 32)], col_r.at[pl.ds(edge + 32, 32)]),
    ]
    near_to = [around[i] for i in (2, 3, 0, 1, 4, 5, 6, 7)]
    near_copies = [
        send(src, dst, (s_near, r_near), i, device)
        for i, ((src, dst), device) in enumerate(zip(near, near_to))
    ]

    low = (lax.broadcasted_iota(jnp.int32, (1, D), 1) < D // 2).astype(F32)
    high = 1.0 - low
    same = (lax.broadcasted_iota(jnp.int32, (D, D), 0) < D // 2) == (
        lax.broadcasted_iota(jnp.int32, (D, D), 1) < D // 2
    )
    ones = jnp.where(same, 1.0, 0.0).astype(BF16)

    def query_scale(layer):
        return (sscale[layer, 0] * low + sscale[layer, 1] * high) * LOG2E

    qkv = dot(norm(x0.reshape(ROWS * COLS, D), again[0:1]).astype(BF16), wqkv[0])
    q = unit(qkv[:, :D], ones) * query_scale(0)
    q0[0] = (q * low).astype(BF16)
    q0[1] = (q * high).astype(BF16)
    k0[pl.ds(96, ROWS * COLS)] = unit(qkv[:, D : 2 * D], ones).astype(BF16)
    v0[pl.ds(96, ROWS * COLS), :D] = qkv[:, 2 * D :].astype(BF16)
    v0[pl.ds(96, ROWS * COLS), D:] = jnp.ones((ROWS * COLS, D), BF16)
    v0[pl.ds(0, 96), D:] = jnp.full((96, D), has_up).astype(BF16)
    v0[pl.ds(96 + ROWS * COLS, 96), D:] = jnp.full((96, D), has_down).astype(BF16)
    for d in range(3):
        flags = jnp.concatenate(
            [
                jnp.full((TRIPS * COLS, D), row_ok[d]),
                jnp.full((TRIPS * WIDE, D), row_ok[d] * has_left),
                jnp.full((TRIPS * WIDE, D), row_ok[d] * has_right),
            ],
            axis=0,
        ).astype(BF16)
        for r in range(STEP):
            v1[r, pl.ds(d * BLOCK, BLOCK), D:] = flags

    for copy in near_copies:
        copy.wait_recv()

    slot = lax.broadcasted_iota(jnp.int32, (32, 8, 1), 1)
    side_row = lax.broadcasted_iota(jnp.int32, (32, 8, 1), 0)
    side_x = jnp.where(
        slot < 4,
        col_r[...].astype(F32).reshape(32, 8, D),
        col_l[...].astype(F32).reshape(32, 8, D),
    )
    side_ok = jnp.where(slot < 4, has_right, has_left) * jnp.where(
        side_row < 4, has_up, jnp.where(side_row < 28, 1.0, has_down)
    )
    halo_x = jnp.concatenate(
        [
            upx[...].astype(F32).reshape(96, D),
            dnx[...].astype(F32).reshape(96, D),
            side_x.reshape(256, D)[8:248],
        ],
        axis=0,
    )
    kv = dot(norm(halo_x, again[0:1]).astype(BF16), wqkv[0, :, D:])
    halo_k = unit(kv[:, :D], ones)
    halo_v = kv[:, D:]
    side_ok = jnp.broadcast_to(side_ok.reshape(256, 1)[8:248], (240, D))
    k0[pl.ds(0, 96)] = halo_k[:96].astype(BF16)
    k0[pl.ds(96 + ROWS * COLS, 96)] = halo_k[96:192].astype(BF16)
    k0s[...] = halo_k[192:].astype(BF16)
    v0[pl.ds(0, 96), :D] = (halo_v[:96] * has_up).astype(BF16)
    v0[pl.ds(96 + ROWS * COLS, 96), :D] = (halo_v[96:192] * has_down).astype(BF16)
    v0s[:, :D] = (halo_v[192:] * side_ok).astype(BF16)
    v0s[:, D:] = side_ok.astype(BF16)

    def attend(query, parts):
        size = query.shape[0] // 2
        total = None
        for key, value, mask in parts:
            weight = jnp.exp2(dot_nt(query, key)).astype(BF16)
            weight = weight.reshape(2, size, -1) * mask[None]
            part = dot(weight.reshape(2 * size, -1), value)
            total = part if total is None else total + part
        numer = total[:size, :D] * low + total[size:, :D] * high
        denom = total[:size, D:] * low + total[size:, D:] * high
        return numer / denom

    def finish(x, attended, layer):
        x1 = x + dot(attended.astype(BF16), wout[layer])
        inner = dot(norm(x1, mgain[layer : layer + 1]).astype(BF16), win[layer])
        value, gate = inner[:, :FF], inner[:, FF:]
        half = 0.5 * gate * value
        hidden = half + half * jnp.tanh(
            gate * (0.7978845608028654 + (0.7978845608028654 * 0.044715) * (gate * gate))
        )
        return x1 + dot(hidden.astype(BF16), wdown[layer])

    def near_layer(j):
        attended = []
        for t in range(TRIPS):
            for pair in range(PER // 2):
                i = STEP * t + PER * j + 2 * pair
                result = attend(
                    q0[:, pl.ds(i * COLS, 64)].reshape(128, D),
                    [
                        (k0[pl.ds(i * COLS, 256)], v0[pl.ds(i * COLS, 256)], mown[...]),
                        (k0s[pl.ds(i * 8, 64)], v0s[pl.ds(i * 8, 64)], mside[...]),
                    ],
                )
                attended += [result[:COLS], result[COLS:]]
        order = [(t * PER + r) for r in range(PER) for t in range(TRIPS)]
        attended = jnp.concatenate([attended[i] for i in order], axis=0)
        x = jnp.concatenate(
            [tok[STEP * t + PER * j + r] for r in range(PER) for t in range(TRIPS)], axis=0
        ).astype(F32)
        x = finish(x, attended, 0)
        x2[j] = x
        h = norm(x, again[1:2])
        h1[j] = h.astype(BF16)
        h = h.reshape(PER * TRIPS, COLS, D)
        hl[j] = h[:, :WIDE].reshape(SIDE, D).astype(BF16)
        hr[j] = h[:, COLS - WIDE :].reshape(SIDE, D).astype(BF16)
        sems = (s_far.at[j], r_far.at[j])
        return [
            send(hr.at[j], lr.at[1, j, pl.ds(0, SIDE)], sems, 0, (row, right)),
            send(hl.at[j], lr.at[1, j, pl.ds(SIDE, SIDE)], sems, 1, (row, left)),
            send(h1.at[j], rc.at[0, j], sems, 2, (down, col)),
            send(h1.at[j], rc.at[1, j], sems, 3, (up, col)),
        ]

    def relay(j, copies):
        copies[0].wait_recv()
        copies[1].wait_recv()
        sems = (s_far.at[j], r_far.at[j])
        copies += [
            send(lr.at[1, j], lr.at[0, j], sems, 4, (down, col)),
            send(lr.at[1, j], lr.at[2, j], sems, 5, (up, col)),
        ]

    def far_layer(j, copies):
        own = h1[j]
        q = unit(dot(own, wqkv[1, :, :D]), ones) * query_scale(1)
        for copy in copies[2:]:
            copy.wait_recv()
        for d in range(3):
            centre = own if d == 1 else rc[d // 2, j]
            kv = dot(jnp.concatenate([centre, lr[d, j]], axis=0), wqkv[1, :, D:])
            key, value = unit(kv[:, :D], ones), kv[:, D:]
            value = jnp.concatenate(
                [
                    value[:TOK] * row_ok[d],
                    value[TOK : TOK + SIDE] * (row_ok[d] * has_left),
                    value[TOK + SIDE :] * (row_ok[d] * has_right),
                ],
                axis=0,
            )
            for r in range(PER):
                for array, ref, lanes in ((key, k1, slice(None)), (value, v1, slice(0, D))):
                    piece = jnp.concatenate(
                        [
                            array[r * 96 : (r + 1) * 96],
                            array[TOK + r * 72 : TOK + (r + 1) * 72],
                            array[TOK + SIDE + r * 72 : TOK + SIDE + (r + 1) * 72],
                        ],
                        axis=0,
                    )
                    ref[PER * j + r, pl.ds(d * BLOCK, BLOCK), lanes] = piece.astype(BF16)
        attended = []
        for r in range(PER):
            part = q[r * 96 : (r + 1) * 96]
            query = jnp.concatenate([part * low, part * high], axis=0).astype(BF16)
            attended.append(attend(query, [(k1[PER * j + r], v1[PER * j + r], mfar[...])]))
        x = finish(x2[j], jnp.concatenate(attended, axis=0), 1).astype(BF16)
        for r in range(PER):
            for t in range(TRIPS):
                at = (r * TRIPS + t) * COLS
                out[STEP * t + PER * j + r] = x[at : at + COLS]

    copies = []
    for j in range(CHUNKS):
        copies.append(near_layer(j))
        if j:
            relay(j - 1, copies[j - 1])
    if CHUNKS == 1:
        relay(0, copies[0])
    for j in range(CHUNKS):
        far_layer(j, copies[j])
        if CHUNKS > 1 and j == 0:
            relay(CHUNKS - 1, copies[-1])
    for copy in near_copies + [c for chunk in copies for c in chunk]:
        copy.wait_send()


def shards(tokens, attn_gain, w_qkv, score_scale, w_out, mlp_gain, w_in, down_weight):
    vmem = pl.BlockSpec(memory_space=pltpu.VMEM)
    smem = pl.BlockSpec(memory_space=pltpu.SMEM)
    own, side = near_masks()
    return pl.pallas_call(
        kernel,
        out_shape=jax.ShapeDtypeStruct((ROWS, COLS, D), BF16),
        in_specs=[vmem, vmem, vmem, smem] + [vmem] * 7,
        out_specs=vmem,
        scratch_shapes=[
            pltpu.VMEM((960, D), BF16),
            pltpu.VMEM((960, 2 * D), BF16),
            pltpu.VMEM((240, D), BF16),
            pltpu.VMEM((240, 2 * D), BF16),
            pltpu.VMEM((2, ROWS * COLS, D), BF16),
            pltpu.VMEM((CHUNKS, TOK, D), F32),
            pltpu.VMEM((3, COLS, D), BF16),
            pltpu.VMEM((3, COLS, D), BF16),
            pltpu.VMEM((ROWS * 8, D), BF16),
            pltpu.VMEM((ROWS * 8, D), BF16),
            pltpu.VMEM((256, D), BF16),
            pltpu.VMEM((256, D), BF16),
            pltpu.VMEM((CHUNKS, TOK, D), BF16),
            pltpu.VMEM((CHUNKS, SIDE, D), BF16),
            pltpu.VMEM((CHUNKS, SIDE, D), BF16),
            pltpu.VMEM((2, CHUNKS, TOK, D), BF16),
            pltpu.VMEM((3, CHUNKS, 2 * SIDE, D), BF16),
            pltpu.VMEM((STEP, 3 * BLOCK, D), BF16),
            pltpu.VMEM((STEP, 3 * BLOCK, 2 * D), BF16),
            pltpu.SemaphoreType.DMA((8,)),
            pltpu.SemaphoreType.DMA((8,)),
            pltpu.SemaphoreType.DMA((CHUNKS, 6)),
            pltpu.SemaphoreType.DMA((CHUNKS, 6)),
        ],
        compiler_params=pltpu.CompilerParams(
            collective_id=0, has_side_effects=True, vmem_limit_bytes=40 * 1024 * 1024
        ),
        name="two_layers",
    )(
        tokens, attn_gain, w_qkv, score_scale, w_out, mlp_gain, w_in, down_weight,
        jnp.asarray(own, BF16), jnp.asarray(side, BF16), jnp.asarray(far_mask(), BF16),
    )


def solution(mesh):
    return jax.shard_map(
        shards,
        mesh=mesh,
        in_specs=(P("row", "col", None), P(), P(), P(), P(), P(), P(), P()),
        out_specs=P("row", "col", None),
        check_vma=False,
    )
```

```python
import jax
import jax.numpy as jnp
from jax import lax
from jax.experimental import pallas as pl
from jax.experimental.pallas import tpu as pltpu
from jax.sharding import PartitionSpec as P

F32, BF16 = jnp.float32, jnp.bfloat16
MESH = pl.DeviceIdType.MESH
D = 128
FF = 384
ROWS, COLS = 24, 32
STEP = 8
TRIPS = ROWS // STEP
WIDE = 24
CHUNKS = 4
PER = STEP // CHUNKS
TOK = PER * TRIPS * COLS
SIDE = PER * TRIPS * WIDE
BLOCK = TRIPS * (COLS + 2 * WIDE)
LOG2E = 1.4426950408889634


def lanes_and_rows(rows, lanes):
    at = lax.broadcasted_iota(jnp.int32, (rows, 1), 0)
    return at >> 5, at & 31, lax.broadcasted_iota(jnp.int32, (1, lanes), 1)


def as_mask(ok):
    return jnp.where(ok, 1.0, 0.0).astype(BF16)


def near_masks():
    a, c, n = lanes_and_rows(64, 256)
    step = (n >> 5) - a
    own = (step >= 0) & (step <= 6) & (abs((n & 31) - c) <= 3)
    a, c, n = lanes_and_rows(64, 64)
    step, slot = (n >> 3) - a, n & 7
    side = (step >= 0) & (step <= 6) & (abs(jnp.where(slot < 4, COLS + slot, slot - 8) - c) <= 3)
    return as_mask(own), as_mask(side)


def far_mask():
    t, c, n = lanes_and_rows(TRIPS * COLS, 3 * BLOCK)
    d = (n >= BLOCK).astype(jnp.int32) + (n >= 2 * BLOCK).astype(jnp.int32)
    n = n - BLOCK * d
    left, right = TRIPS * COLS, TRIPS * (COLS + WIDE)
    m = jnp.where(n >= right, n - right, n - left)
    t2 = (m >= WIDE).astype(jnp.int32) + (m >= 2 * WIDE).astype(jnp.int32)
    m = m - WIDE * t2 + jnp.where(n >= right, COLS, -WIDE)
    key_col = jnp.where(n < left, n & 31, m)
    key_row = TRIPS * (d - 1) + jnp.where(n < left, n >> 5, t2)
    step = key_col - c
    return as_mask(
        (abs(key_row - t) <= 3) & ((step & (STEP - 1)) == 0) & (abs(step) <= 3 * STEP)
    )


def dot(a, b):
    return jnp.dot(a, b, preferred_element_type=F32)


def dot_nt(a, b):
    return lax.dot_general(a, b, (((1,), (1,)), ((), ())), preferred_element_type=F32)


def norm(x, gain):
    return x * lax.rsqrt(jnp.mean(x * x, axis=-1, keepdims=True) + 1e-6) * gain


def unit(x, ones):
    return x * lax.rsqrt(dot((x * x).astype(BF16), ones) + 1e-6)


OPERANDS = 8


def kernel(*refs):
    body(refs[:OPERANDS], *refs[OPERANDS:])


def body(
    given, out,
    tok, again, wqkv, sscale, wout, mgain, win, wdown, s_given, mown, mside, mfar,
    k0, v0, k0s, v0s, q0, x2, upx, dnx, pack_l, pack_r, col_l, col_r,
    h1, hl, hr, rc, lr, k1, v1, s_near, r_near, s_far, r_far,
):
    row, col = lax.axis_index("row"), lax.axis_index("col")
    n_row, n_col = lax.axis_size("row"), lax.axis_size("col")
    up, down = lax.rem(row + n_row - 1, n_row), lax.rem(row + 1, n_row)
    left, right = lax.rem(col + n_col - 1, n_col), lax.rem(col + 1, n_col)

    own = (tok, again, wqkv, sscale, wout, mgain, win, wdown)
    fetches = [
        pltpu.make_async_copy(src, dst, s_given.at[i])
        for i, (src, dst) in enumerate(zip(given, own))
    ]
    for fetch in fetches:
        fetch.start()

    barrier = pltpu.get_barrier_semaphore()
    around = [
        (down, col), (up, col), (row, right), (row, left),
        (down, right), (up, right), (down, left), (up, left),
    ]
    for device in around:
        pl.semaphore_signal(barrier, inc=1, device_id=device, device_id_type=MESH)

    has_up = (row > 0).astype(F32)
    has_down = (row < n_row - 1).astype(F32)
    has_left = (col > 0).astype(F32)
    has_right = (col < n_col - 1).astype(F32)
    row_ok = (has_up, jnp.float32(1), has_down)

    mown[...], mside[...] = near_masks()
    mfar[...] = far_mask()

    fetches[0].wait()
    x0 = tok[...].astype(F32)
    pack_l[...] = x0[:, :8].reshape(ROWS * 8, D).astype(BF16)
    pack_r[...] = x0[:, COLS - 8 :].reshape(ROWS * 8, D).astype(BF16)

    pl.semaphore_wait(barrier, 8)

    def send(src, dst, sems, at, device):
        copy = pltpu.make_async_remote_copy(
            src_ref=src, dst_ref=dst, send_sem=sems[0].at[at], recv_sem=sems[1].at[at],
            device_id=device, device_id_type=MESH,
        )
        copy.start()
        return copy

    edge = ROWS * 8
    near = [
        (pack_r, col_l.at[pl.ds(32, edge)]),
        (pack_l, col_r.at[pl.ds(32, edge)]),
        (given[0].at[pl.ds(ROWS - 3, 3)], upx),
        (given[0].at[pl.ds(0, 3)], dnx),
        (pack_r.at[pl.ds(edge - 32, 32)], col_l.at[pl.ds(0, 32)]),
        (pack_r.at[pl.ds(0, 32)], col_l.at[pl.ds(edge + 32, 32)]),
        (pack_l.at[pl.ds(edge - 32, 32)], col_r.at[pl.ds(0, 32)]),
        (pack_l.at[pl.ds(0, 32)], col_r.at[pl.ds(edge + 32, 32)]),
    ]
    near_to = [around[i] for i in (2, 3, 0, 1, 4, 5, 6, 7)]
    near_copies = [
        send(src, dst, (s_near, r_near), i, device)
        for i, ((src, dst), device) in enumerate(zip(near, near_to))
    ]

    low = (lax.broadcasted_iota(jnp.int32, (1, D), 1) < D // 2).astype(F32)
    high = 1.0 - low
    same = (lax.broadcasted_iota(jnp.int32, (D, D), 0) < D // 2) == (
        lax.broadcasted_iota(jnp.int32, (D, D), 1) < D // 2
    )
    ones = jnp.where(same, 1.0, 0.0).astype(BF16)

    def query_scale(layer):
        scale = sscale[layer : layer + 1]
        return (scale[:, :1] * low + scale[:, 1:] * high) * LOG2E

    for fetch in fetches[1:]:
        fetch.wait()

    qkv = dot(norm(x0.reshape(ROWS * COLS, D), again[0:1]).astype(BF16), wqkv[0])
    q = unit(qkv[:, :D], ones) * query_scale(0)
    q0[0] = (q * low).astype(BF16)
    q0[1] = (q * high).astype(BF16)
    k0[pl.ds(96, ROWS * COLS)] = unit(qkv[:, D : 2 * D], ones).astype(BF16)
    v0[pl.ds(96, ROWS * COLS), :D] = qkv[:, 2 * D :].astype(BF16)
    v0[pl.ds(96, ROWS * COLS), D:] = jnp.ones((ROWS * COLS, D), BF16)
    v0[pl.ds(0, 96), D:] = jnp.full((96, D), has_up).astype(BF16)
    v0[pl.ds(96 + ROWS * COLS, 96), D:] = jnp.full((96, D), has_down).astype(BF16)
    for d in range(3):
        flags = jnp.concatenate(
            [
                jnp.full((TRIPS * COLS, D), row_ok[d]),
                jnp.full((TRIPS * WIDE, D), row_ok[d] * has_left),
                jnp.full((TRIPS * WIDE, D), row_ok[d] * has_right),
            ],
            axis=0,
        ).astype(BF16)
        for r in range(STEP):
            v1[r, pl.ds(d * BLOCK, BLOCK), D:] = flags

    for copy in near_copies:
        copy.wait_recv()

    slot = lax.broadcasted_iota(jnp.int32, (32, 8, 1), 1)
    side_row = lax.broadcasted_iota(jnp.int32, (32, 8, 1), 0)
    side_x = jnp.where(
        slot < 4,
        col_r[...].astype(F32).reshape(32, 8, D),
        col_l[...].astype(F32).reshape(32, 8, D),
    )
    side_ok = jnp.where(slot < 4, has_right, has_left) * jnp.where(
        side_row < 4, has_up, jnp.where(side_row < 28, 1.0, has_down)
    )
    halo_x = jnp.concatenate(
        [
            upx[...].astype(F32).reshape(96, D),
            dnx[...].astype(F32).reshape(96, D),
            side_x.reshape(256, D)[8:248],
        ],
        axis=0,
    )
    kv = dot(norm(halo_x, again[0:1]).astype(BF16), wqkv[0, :, D:])
    halo_k = unit(kv[:, :D], ones)
    halo_v = kv[:, D:]
    side_ok = jnp.broadcast_to(side_ok.reshape(256, 1)[8:248], (240, D))
    k0[pl.ds(0, 96)] = halo_k[:96].astype(BF16)
    k0[pl.ds(96 + ROWS * COLS, 96)] = halo_k[96:192].astype(BF16)
    k0s[...] = halo_k[192:].astype(BF16)
    v0[pl.ds(0, 96), :D] = (halo_v[:96] * has_up).astype(BF16)
    v0[pl.ds(96 + ROWS * COLS, 96), :D] = (halo_v[96:192] * has_down).astype(BF16)
    v0s[:, :D] = (halo_v[192:] * side_ok).astype(BF16)
    v0s[:, D:] = side_ok.astype(BF16)

    def attend(query, parts):
        size = query.shape[0] // 2
        total = None
        for key, value, mask in parts:
            weight = jnp.exp2(dot_nt(query, key)).astype(BF16)
            weight = weight.reshape(2, size, -1) * mask[None]
            part = dot(weight.reshape(2 * size, -1), value)
            total = part if total is None else total + part
        numer = total[:size, :D] * low + total[size:, :D] * high
        denom = total[:size, D:] * low + total[size:, D:] * high
        return numer / denom

    def finish(x, attended, layer):
        x1 = x + dot(attended.astype(BF16), wout[layer])
        inner = dot(norm(x1, mgain[layer : layer + 1]).astype(BF16), win[layer])
        value, gate = inner[:, :FF], inner[:, FF:]
        half = 0.5 * gate * value
        hidden = half + half * jnp.tanh(
            gate * (0.7978845608028654 + (0.7978845608028654 * 0.044715) * (gate * gate))
        )
        return x1 + dot(hidden.astype(BF16), wdown[layer])

    def near_layer(j):
        attended = []
        for t in range(TRIPS):
            for pair in range(PER // 2):
                i = STEP * t + PER * j + 2 * pair
                result = attend(
                    q0[:, pl.ds(i * COLS, 64)].reshape(128, D),
                    [
                        (k0[pl.ds(i * COLS, 256)], v0[pl.ds(i * COLS, 256)], mown[...]),
                        (k0s[pl.ds(i * 8, 64)], v0s[pl.ds(i * 8, 64)], mside[...]),
                    ],
                )
                attended += [result[:COLS], result[COLS:]]
        order = [(t * PER + r) for r in range(PER) for t in range(TRIPS)]
        attended = jnp.concatenate([attended[i] for i in order], axis=0)
        x = jnp.concatenate(
            [tok[STEP * t + PER * j + r] for r in range(PER) for t in range(TRIPS)], axis=0
        ).astype(F32)
        x = finish(x, attended, 0)
        x2[j] = x
        h = norm(x, again[1:2])
        h1[j] = h.astype(BF16)
        h = h.reshape(PER * TRIPS, COLS, D)
        hl[j] = h[:, :WIDE].reshape(SIDE, D).astype(BF16)
        hr[j] = h[:, COLS - WIDE :].reshape(SIDE, D).astype(BF16)
        sems = (s_far.at[j], r_far.at[j])
        return [
            send(hr.at[j], lr.at[1, j, pl.ds(0, SIDE)], sems, 0, (row, right)),
            send(hl.at[j], lr.at[1, j, pl.ds(SIDE, SIDE)], sems, 1, (row, left)),
            send(h1.at[j], rc.at[0, j], sems, 2, (down, col)),
            send(h1.at[j], rc.at[1, j], sems, 3, (up, col)),
        ]

    def relay(j, copies):
        copies[0].wait_recv()
        copies[1].wait_recv()
        sems = (s_far.at[j], r_far.at[j])
        copies += [
            send(lr.at[1, j], lr.at[0, j], sems, 4, (down, col)),
            send(lr.at[1, j], lr.at[2, j], sems, 5, (up, col)),
        ]

    def far_layer(j, copies):
        own = h1[j]
        q = unit(dot(own, wqkv[1, :, :D]), ones) * query_scale(1)
        for copy in copies[2:]:
            copy.wait_recv()
        for d in range(3):
            centre = own if d == 1 else rc[d // 2, j]
            kv = dot(jnp.concatenate([centre, lr[d, j]], axis=0), wqkv[1, :, D:])
            key, value = unit(kv[:, :D], ones), kv[:, D:]
            value = jnp.concatenate(
                [
                    value[:TOK] * row_ok[d],
                    value[TOK : TOK + SIDE] * (row_ok[d] * has_left),
                    value[TOK + SIDE :] * (row_ok[d] * has_right),
                ],
                axis=0,
            )
            for r in range(PER):
                for array, ref, lanes in ((key, k1, slice(None)), (value, v1, slice(0, D))):
                    piece = jnp.concatenate(
                        [
                            array[r * 96 : (r + 1) * 96],
                            array[TOK + r * 72 : TOK + (r + 1) * 72],
                            array[TOK + SIDE + r * 72 : TOK + SIDE + (r + 1) * 72],
                        ],
                        axis=0,
                    )
                    ref[PER * j + r, pl.ds(d * BLOCK, BLOCK), lanes] = piece.astype(BF16)
        attended = []
        for r in range(PER):
            part = q[r * 96 : (r + 1) * 96]
            query = jnp.concatenate([part * low, part * high], axis=0).astype(BF16)
            attended.append(attend(query, [(k1[PER * j + r], v1[PER * j + r], mfar[...])]))
        x = finish(x2[j], jnp.concatenate(attended, axis=0), 1).astype(BF16)
        for r in range(PER):
            for t in range(TRIPS):
                at = (r * TRIPS + t) * COLS
                out[STEP * t + PER * j + r] = x[at : at + COLS]

    copies = []
    for j in range(CHUNKS):
        copies.append(near_layer(j))
        if j:
            relay(j - 1, copies[j - 1])
    if CHUNKS == 1:
        relay(0, copies[0])
    for j in range(CHUNKS):
        far_layer(j, copies[j])
        if CHUNKS > 1 and j == 0:
            relay(CHUNKS - 1, copies[-1])
    for copy in near_copies + [c for chunk in copies for c in chunk]:
        copy.wait_send()


def shards(tokens, attn_gain, w_qkv, score_scale, w_out, mlp_gain, w_in, down_weight):
    operands = (tokens, attn_gain, w_qkv, score_scale, w_out, mlp_gain, w_in, down_weight)
    return pl.pallas_call(
        kernel,
        out_shape=jax.ShapeDtypeStruct((ROWS, COLS, D), BF16),
        in_specs=[pl.BlockSpec(memory_space=pltpu.HBM)] * OPERANDS,
        out_specs=pl.BlockSpec(memory_space=pltpu.VMEM),
        scratch_shapes=[pltpu.VMEM(a.shape, a.dtype) for a in operands]
        + [
            pltpu.SemaphoreType.DMA((OPERANDS,)),
            pltpu.VMEM((64, 256), BF16),
            pltpu.VMEM((64, 64), BF16),
            pltpu.VMEM((TRIPS * COLS, 3 * BLOCK), BF16),
            pltpu.VMEM((960, D), BF16),
            pltpu.VMEM((960, 2 * D), BF16),
            pltpu.VMEM((240, D), BF16),
            pltpu.VMEM((240, 2 * D), BF16),
            pltpu.VMEM((2, ROWS * COLS, D), BF16),
            pltpu.VMEM((CHUNKS, TOK, D), F32),
            pltpu.VMEM((3, COLS, D), BF16),
            pltpu.VMEM((3, COLS, D), BF16),
            pltpu.VMEM((ROWS * 8, D), BF16),
            pltpu.VMEM((ROWS * 8, D), BF16),
            pltpu.VMEM((256, D), BF16),
            pltpu.VMEM((256, D), BF16),
            pltpu.VMEM((CHUNKS, TOK, D), BF16),
            pltpu.VMEM((CHUNKS, SIDE, D), BF16),
            pltpu.VMEM((CHUNKS, SIDE, D), BF16),
            pltpu.VMEM((2, CHUNKS, TOK, D), BF16),
            pltpu.VMEM((3, CHUNKS, 2 * SIDE, D), BF16),
            pltpu.VMEM((STEP, 3 * BLOCK, D), BF16),
            pltpu.VMEM((STEP, 3 * BLOCK, 2 * D), BF16),
            pltpu.SemaphoreType.DMA((8,)),
            pltpu.SemaphoreType.DMA((8,)),
            pltpu.SemaphoreType.DMA((CHUNKS, 6)),
            pltpu.SemaphoreType.DMA((CHUNKS, 6)),
        ],
        compiler_params=pltpu.CompilerParams(
            collective_id=0, has_side_effects=True, vmem_limit_bytes=60 * 1024 * 1024
        ),
        name="two_layers",
    )(*operands)


def solution(mesh):
    return jax.shard_map(
        shards,
        mesh=mesh,
        in_specs=(P("row", "col", None), P(), P(), P(), P(), P(), P(), P()),
        out_specs=P("row", "col", None),
        check_vma=False,
    )
```

```python
import jax
import jax.numpy as jnp
from jax import lax
from jax.experimental import pallas as pl
from jax.experimental.pallas import tpu as pltpu
from jax.sharding import PartitionSpec as P

F32, BF16 = jnp.float32, jnp.bfloat16
MESH = pl.DeviceIdType.MESH
D = 128
FF = 384
ROWS, COLS = 24, 32
STEP = 8
TRIPS = ROWS // STEP
WIDE = 24
ROWS_OF = ((3, 11, 19, 4, 12, 20), (9, 17, 10, 18, 1, 2), (5, 13, 6, 14, 21, 22), (7, 15, 8, 16, 23, 0))
BATCHES = (
    (((3, 4), (11, 12), (19, 20)), ((0, 0, 6),)),
    (((9, 10), (17, 18), (5, 6), (13, 14), (7, 8), (15, 16)), ((1, 0, 4), (2, 0, 4), (3, 0, 4))),
    (((1, 2), (21, 22), (23,), (0,)), ((1, 4, 2), (2, 4, 2), (3, 4, 2))),
)
CHUNKS = 4
PER = STEP // CHUNKS
TOK = PER * TRIPS * COLS
SIDE = PER * TRIPS * WIDE
BLOCK = TRIPS * (COLS + 2 * WIDE)
LOG2E = 1.4426950408889634


def lanes_and_rows(rows, lanes):
    at = lax.broadcasted_iota(jnp.int32, (rows, 1), 0)
    return at >> 5, at & 31, lax.broadcasted_iota(jnp.int32, (1, lanes), 1)


def as_mask(ok):
    return jnp.where(ok, 1.0, 0.0).astype(BF16)


def row_mask(first, rows, queries=2):
    a, c, n = lanes_and_rows(queries * COLS, rows * COLS)
    step = (n >> 5) + first - a
    return as_mask((step >= 0) & (step <= 6) & (abs((n & 31) - c) <= 3))


def side_mask(first, queries=2):
    a, c, n = lanes_and_rows(queries * COLS, 64)
    step = 2 * (n >> 4) + ((n >> 2) & 1) + first - a
    at = (n & 3) + jnp.where((n & 8) == 0, -4, COLS)
    return as_mask((step >= 0) & (step <= 6) & (abs(at - c) <= 3))


def far_mask():
    t, c, n = lanes_and_rows(TRIPS * COLS, 3 * BLOCK)
    first = (n >= BLOCK).astype(jnp.int32)
    second = (n >= 2 * BLOCK).astype(jnp.int32)
    n = n - BLOCK * (first + second)
    left, right = TRIPS * COLS, TRIPS * (COLS + WIDE)
    m = jnp.where(n >= right, n - right, n - left)
    t2 = (m >= WIDE).astype(jnp.int32) + (m >= 2 * WIDE).astype(jnp.int32)
    m = m - WIDE * t2 + jnp.where(n >= right, COLS, -WIDE)
    key_col = jnp.where(n < left, n & 31, m)
    key_row = TRIPS * (2 * second - first) + jnp.where(n < left, n >> 5, t2)
    step = key_col - c
    return as_mask(
        (abs(key_row - t) <= 3) & ((step & (STEP - 1)) == 0) & (abs(step) <= 3 * STEP)
    )


def dot(a, b):
    return jnp.dot(a, b, preferred_element_type=F32)


def dot_nt(a, b):
    return lax.dot_general(a, b, (((1,), (1,)), ((), ())), preferred_element_type=F32)


def norm(x, gain):
    return x * lax.rsqrt(jnp.mean(x * x, axis=-1, keepdims=True) + 1e-6) * gain


def unit(x, ones):
    return x * lax.rsqrt(dot((x * x).astype(BF16), ones) + 1e-6)


OPERANDS = 8


def kernel(*refs):
    body(refs[:OPERANDS], *refs[OPERANDS:])


def body(
    given, out,
    tok, again, wqkv, sscale, wout, mgain, win, wdown, s_given, mown, mside, mfar,
    k0, v0, k0e, v0e, k0s, v0s, q0, acc0, x2, upx, dnx, pack_l, pack_r, beside,
    h1, hl, hr, rc, lr, q1, k1, v1, acc1, s_near, r_near, s_far, r_far,
):
    row, col = lax.axis_index("row"), lax.axis_index("col")
    n_row, n_col = lax.axis_size("row"), lax.axis_size("col")
    up, down = lax.rem(row + n_row - 1, n_row), lax.rem(row + 1, n_row)
    left, right = lax.rem(col + n_col - 1, n_col), lax.rem(col + 1, n_col)

    own = (tok, again, wqkv, sscale, wout, mgain, win, wdown)
    fetches = [
        pltpu.make_async_copy(src, dst, s_given.at[i])
        for i, (src, dst) in enumerate(zip(given, own))
    ]
    for fetch in fetches:
        fetch.start()

    barrier = pltpu.get_barrier_semaphore()
    around = [(down, col), (up, col), (row, right), (row, left)]
    for device in around:
        pl.semaphore_signal(barrier, inc=1, device_id=device, device_id_type=MESH)

    has_up = (row > 0).astype(F32)
    has_down = (row < n_row - 1).astype(F32)
    has_left = (col > 0).astype(F32)
    has_right = (col < n_col - 1).astype(F32)
    row_ok = (jnp.float32(1), has_up, has_down)

    mown[...] = row_mask(0, 8)
    mside[...] = side_mask(0)
    mfar[...] = far_mask()

    fetches[0].wait()
    x0 = tok[...].astype(F32)
    even, odd = (x0.reshape(ROWS // 2, 2, COLS, D)[:, i] for i in range(2))
    slot = lax.broadcasted_iota(jnp.int32, (1, 8, 1), 1) < 4
    pack_l[...] = (
        jnp.where(slot, even[:, :8], pltpu.roll(odd[:, :8], 4, 1)).reshape(96, D).astype(BF16)
    )
    pack_r[...] = (
        jnp.where(slot, pltpu.roll(even[:, COLS - 8 :], 4, 1), odd[:, COLS - 8 :])
        .reshape(96, D)
        .astype(BF16)
    )

    def send(src, dst, sems, at, device):
        copy = pltpu.make_async_remote_copy(
            src_ref=src, dst_ref=dst, send_sem=sems[0].at[at], recv_sem=sems[1].at[at],
            device_id=device, device_id_type=MESH,
        )
        copy.start()
        return copy

    lane = lax.broadcasted_iota(jnp.int32, (1, 2 * D), 1)
    first_head = (lane & (D // 2)) == 0
    low = jnp.where(first_head[:, :D], 1.0, 0.0)
    high = 1.0 - low
    same = (lax.broadcasted_iota(jnp.int32, (D, D), 0) < D // 2) == (
        lax.broadcasted_iota(jnp.int32, (D, D), 1) < D // 2
    )
    ones = jnp.where(same, 1.0, 0.0).astype(BF16)

    def query_scale(layer):
        scale = sscale[layer : layer + 1]
        return (scale[:, :1] * low + scale[:, 1:] * high) * LOG2E

    for fetch in fetches[1:]:
        fetch.wait()

    def attend(query, parts):
        size = query.shape[0] // 2
        total = None
        for key, value, mask in parts:
            weight = jnp.exp2(dot_nt(query, key)).astype(BF16)
            weight = weight.reshape(2, size, -1) * mask[None]
            part = dot(weight.reshape(2 * size, -1), value)
            total = part if total is None else total + part
        return jnp.where(first_head, total[:size], total[size:])

    qkv = dot(norm(x0.reshape(ROWS * COLS, D), again[0:1]).astype(BF16), wqkv[0])
    q = unit(qkv[:, :D], ones) * query_scale(0)
    q0[0] = (q * low).astype(BF16)
    q0[1] = (q * high).astype(BF16)
    k0[...] = unit(qkv[:, D : 2 * D], ones).astype(BF16)
    v0[:, :D] = qkv[:, 2 * D :].astype(BF16)
    v0[:, D:] = jnp.ones((ROWS * COLS, D), BF16)

    pl.semaphore_wait(barrier, 4)
    near = (s_near, r_near)
    near_copies = [
        send(pack_r, beside.at[0, pl.ds(16, 96)], near, 0, (row, right)),
        send(pack_l, beside.at[1, pl.ds(16, 96)], near, 1, (row, left)),
        send(given[0].at[pl.ds(ROWS - 3, 3)], upx, near, 2, (down, col)),
        send(given[0].at[pl.ds(0, 3)], dnx, near, 3, (up, col)),
    ]

    def query_of(rows):
        size = len(rows) * COLS
        return q0[:, pl.ds(rows[0] * COLS, size)].reshape(2 * size, D)

    for groups, _ in BATCHES:
        for rows in groups:
            i, end = rows[0], min(rows[-1] + 4, ROWS)
            begin = max(i - 3, 0)
            keys = pl.ds(begin * COLS, (end - begin) * COLS)
            whole = end - begin == 8
            mask = mown[...] if whole else row_mask(begin - i + 3, end - begin, len(rows))
            acc0[pl.ds(i * COLS, len(rows) * COLS)] = attend(
                query_of(rows), [(k0[keys], v0[keys], mask)]
            )
    v0e[pl.ds(0, 96), D:] = jnp.full((96, D), has_up).astype(BF16)
    v0e[pl.ds(96, 96), D:] = jnp.full((96, D), has_down).astype(BF16)
    for d in range(3):
        flags = jnp.concatenate(
            [
                jnp.full((TRIPS * COLS, D), row_ok[d]),
                jnp.full((TRIPS * WIDE, D), row_ok[d] * has_left),
                jnp.full((TRIPS * WIDE, D), row_ok[d] * has_right),
            ],
            axis=0,
        ).astype(BF16)
        for r in range(STEP):
            v1[r, pl.ds(d * BLOCK, BLOCK), D:] = flags

    def halo_keys(x):
        kv = dot(norm(x, again[0:1]).astype(BF16), wqkv[0, :, D:])
        return unit(kv[:, :D], ones).astype(BF16), kv[:, D:]

    def side_tokens(at, size):
        both = [beside[i, pl.ds(at, size)].astype(F32).reshape(size // 8, 8, D) for i in range(2)]
        return jnp.stack(both, axis=1).reshape(2 * size, D)

    def side_ok(size, flag):
        at = lax.broadcasted_iota(jnp.int32, (size, D), 0)
        return jnp.where((at & 8) == 0, has_left, has_right) * flag

    for copy in near_copies[:2]:
        copy.wait_recv()
    near_copies += [
        send(beside.at[:, pl.ds(96, 16)], beside.at[:, pl.ds(0, 16)], near, 4, (down, col)),
        send(beside.at[:, pl.ds(16, 16)], beside.at[:, pl.ds(112, 16)], near, 5, (up, col)),
    ]
    key, value = halo_keys(side_tokens(16, 96))
    k0s[pl.ds(32, 192)] = key
    ok = side_ok(192, 1.0)
    v0s[pl.ds(32, 192), :D] = (value * ok).astype(BF16)
    v0s[pl.ds(32, 192), D:] = ok.astype(BF16)

    def far_halo():
        for copy in near_copies[2:]:
            copy.wait_recv()
        x = jnp.concatenate(
            [
                upx[...].astype(F32).reshape(96, D),
                dnx[...].astype(F32).reshape(96, D),
                side_tokens(0, 16),
                side_tokens(112, 16),
            ],
            axis=0,
        )
        key, value = halo_keys(x)
        k0e[...] = key[:192]
        v0e[pl.ds(0, 96), :D] = (value[:96] * has_up).astype(BF16)
        v0e[pl.ds(96, 96), :D] = (value[96:192] * has_down).astype(BF16)
        for at, place, flag in ((192, 0, has_up), (224, 224, has_down)):
            ok = side_ok(32, flag)
            k0s[pl.ds(place, 32)] = key[at : at + 32]
            v0s[pl.ds(place, 32), :D] = (value[at : at + 32] * ok).astype(BF16)
            v0s[pl.ds(place, 32), D:] = ok.astype(BF16)

    def finish(x, attended, layer):
        x1 = x + dot(attended.astype(BF16), wout[layer])
        inner = dot(norm(x1, mgain[layer : layer + 1]).astype(BF16), win[layer])
        value, gate = inner[:, :FF], inner[:, FF:]
        half = 0.5 * gate * value
        hidden = half + half * jnp.tanh(
            gate * (0.7978845608028654 + (0.7978845608028654 * 0.044715) * (gate * gate))
        )
        return x1 + dot(hidden.astype(BF16), wdown[layer])

    sides = [[] for _ in range(CHUNKS)]
    centres = [[] for _ in range(CHUNKS)]
    relays = [[] for _ in range(CHUNKS)]

    def near_layer(groups, pieces):
        attended = {}
        for rows in groups:
            i = rows[0]
            first = 2 * ((i + 1) // 2) - 4
            keys = pl.ds((i + 1) // 2 * 16, 64)
            whole = len(rows) == 2
            mask = mside[...] if whole else side_mask(first - i + 3, 1)
            parts = [(k0s[keys], v0s[keys], mask)]
            if i < 3:
                parts.append((k0e[pl.ds(0, 96)], v0e[pl.ds(0, 96)], row_mask(-i, 3, len(rows))))
            if rows[-1] + 4 > ROWS:
                mask = row_mask(ROWS + 3 - i, 3, len(rows))
                parts.append((k0e[pl.ds(96, 96)], v0e[pl.ds(96, 96)], mask))
            result = acc0[pl.ds(i * COLS, len(rows) * COLS)] + attend(query_of(rows), parts)
            result = result[:, :D] / result[:, D:]
            for at, one in enumerate(rows):
                attended[one] = result[at * COLS : (at + 1) * COLS]
        order = [ROWS_OF[j][p] for j, start, size in pieces for p in range(start, start + size)]
        x = jnp.concatenate([tok[i] for i in order], axis=0).astype(F32)
        x = finish(x, jnp.concatenate([attended[i] for i in order], axis=0), 0)
        h = norm(x, again[1:2])
        at = 0
        for j, start, size in pieces:
            whole = pl.ds(start * COLS, size * COLS)
            part = pl.ds(start * WIDE, size * WIDE)
            rows = slice(at, at + size * COLS)
            at += size * COLS
            piece = h[rows].reshape(size, COLS, D)
            hl[j, part] = piece[:, :WIDE].reshape(size * WIDE, D).astype(BF16)
            hr[j, part] = piece[:, COLS - WIDE :].reshape(size * WIDE, D).astype(BF16)
            h1[j, whole] = h[rows].astype(BF16)
            x2[j, whole] = x[rows]
        for j, start, size in pieces:
            part = pl.ds(start * WIDE, size * WIDE)
            other = pl.ds(SIDE + start * WIDE, size * WIDE)
            sems = (s_far.at[j], r_far.at[j])
            k = 0 if start == 0 else 2
            sides[j] += [
                send(hr.at[j, part], lr.at[0, j, part], sems, k, (row, right)),
                send(hl.at[j, part], lr.at[0, j, other], sems, k + 1, (row, left)),
            ]
        for j, start, size in pieces:
            whole = pl.ds(start * COLS, size * COLS)
            sems = (s_far.at[j], r_far.at[j])
            k = 4 if start == 0 else 6
            centres[j] += [
                send(h1.at[j, whole], rc.at[0, j, whole], sems, k, (down, col)),
                send(h1.at[j, whole], rc.at[1, j, whole], sems, k + 1, (up, col)),
            ]

    def relay(j):
        for copy in sides[j]:
            copy.wait_recv()
        sems = (s_far.at[j], r_far.at[j])
        relays[j] += [
            send(lr.at[0, j], lr.at[1, j], sems, 8, (down, col)),
            send(lr.at[0, j], lr.at[2, j], sems, 9, (up, col)),
        ]

    def residues(j):
        firsts = sorted({i % STEP for i in ROWS_OF[j]})
        return [[ROWS_OF[j].index(i + STEP * t) for t in range(TRIPS)] for i in firsts]

    def far_keys(j, d):
        centre = h1[j] if d == 0 else rc[d - 1, j]
        kv = dot(jnp.concatenate([centre, lr[d, j]], axis=0), wqkv[1, :, D:])
        key, value = unit(kv[:, :D], ones), kv[:, D:]
        value = jnp.concatenate(
            [
                value[:TOK] * row_ok[d],
                value[TOK : TOK + SIDE] * (row_ok[d] * has_left),
                value[TOK + SIDE :] * (row_ok[d] * has_right),
            ],
            axis=0,
        )
        for r, places in enumerate(residues(j)):
            for array, ref, lanes in ((key, k1, slice(None)), (value, v1, slice(0, D))):
                piece = jnp.concatenate(
                    [array[p * COLS : (p + 1) * COLS] for p in places]
                    + [
                        array[base + p * WIDE : base + (p + 1) * WIDE]
                        for base in (TOK, TOK + SIDE)
                        for p in places
                    ],
                    axis=0,
                )
                ref[PER * j + r, pl.ds(d * BLOCK, BLOCK), lanes] = piece.astype(BF16)

    def far_own(j):
        q = unit(dot(h1[j], wqkv[1, :, :D]), ones) * query_scale(1)
        far_keys(j, 0)
        for r, places in enumerate(residues(j)):
            part = jnp.concatenate([q[p * COLS : (p + 1) * COLS] for p in places], axis=0)
            query = jnp.concatenate([part * low, part * high], axis=0).astype(BF16)
            q1[PER * j + r] = query
            keys = (PER * j + r, pl.ds(0, BLOCK))
            acc1[PER * j + r] = attend(query, [(k1[keys], v1[keys], mfar[:, :BLOCK])])

    def far_layer(j):
        for copy in centres[j] + relays[j]:
            copy.wait_recv()
        far_keys(j, 1)
        far_keys(j, 2)
        attended = [None] * len(ROWS_OF[j])
        for r, places in enumerate(residues(j)):
            keys = (PER * j + r, pl.ds(BLOCK, 2 * BLOCK))
            result = acc1[PER * j + r] + attend(
                q1[PER * j + r], [(k1[keys], v1[keys], mfar[:, BLOCK:])]
            )
            result = result[:, :D] / result[:, D:]
            for t, p in enumerate(places):
                attended[p] = result[t * COLS : (t + 1) * COLS]
        x = finish(x2[j], jnp.concatenate(attended, axis=0), 1).astype(BF16)
        for p, i in enumerate(ROWS_OF[j]):
            out[i] = x[p * COLS : (p + 1) * COLS]

    near_layer(*BATCHES[0])
    near_layer(*BATCHES[1])
    far_halo()
    near_layer(*BATCHES[2])
    for j in range(CHUNKS):
        relay(j)
        far_own(j)
    for j in range(CHUNKS):
        far_layer(j)
    for copy in near_copies + sum(sides + centres + relays, []):
        copy.wait_send()


def shards(tokens, attn_gain, w_qkv, score_scale, w_out, mlp_gain, w_in, down_weight):
    operands = (tokens, attn_gain, w_qkv, score_scale, w_out, mlp_gain, w_in, down_weight)
    operands = [pltpu.with_memory_space_constraint(a, pltpu.HBM) for a in operands]
    return pl.pallas_call(
        kernel,
        out_shape=jax.ShapeDtypeStruct((ROWS, COLS, D), BF16),
        in_specs=[pl.BlockSpec(memory_space=pltpu.HBM)] * OPERANDS,
        out_specs=pl.BlockSpec(memory_space=pltpu.VMEM),
        scratch_shapes=[pltpu.VMEM(a.shape, a.dtype) for a in operands]
        + [
            pltpu.SemaphoreType.DMA((OPERANDS,)),
            pltpu.VMEM((64, 256), BF16),
            pltpu.VMEM((64, 64), BF16),
            pltpu.VMEM((TRIPS * COLS, 3 * BLOCK), BF16),
            pltpu.VMEM((ROWS * COLS, D), BF16),
            pltpu.VMEM((ROWS * COLS, 2 * D), BF16),
            pltpu.VMEM((192, D), BF16),
            pltpu.VMEM((192, 2 * D), BF16),
            pltpu.VMEM((256, D), BF16),
            pltpu.VMEM((256, 2 * D), BF16),
            pltpu.VMEM((2, ROWS * COLS, D), BF16),
            pltpu.VMEM((ROWS * COLS, 2 * D), F32),
            pltpu.VMEM((CHUNKS, TOK, D), F32),
            pltpu.VMEM((3, COLS, D), BF16),
            pltpu.VMEM((3, COLS, D), BF16),
            pltpu.VMEM((96, D), BF16),
            pltpu.VMEM((96, D), BF16),
            pltpu.VMEM((2, 128, D), BF16),
            pltpu.VMEM((CHUNKS, TOK, D), BF16),
            pltpu.VMEM((CHUNKS, SIDE, D), BF16),
            pltpu.VMEM((CHUNKS, SIDE, D), BF16),
            pltpu.VMEM((2, CHUNKS, TOK, D), BF16),
            pltpu.VMEM((3, CHUNKS, 2 * SIDE, D), BF16),
            pltpu.VMEM((STEP, 2 * TRIPS * COLS, D), BF16),
            pltpu.VMEM((STEP, 3 * BLOCK, D), BF16),
            pltpu.VMEM((STEP, 3 * BLOCK, 2 * D), BF16),
            pltpu.VMEM((STEP, TRIPS * COLS, 2 * D), F32),
            pltpu.SemaphoreType.DMA((6,)),
            pltpu.SemaphoreType.DMA((6,)),
            pltpu.SemaphoreType.DMA((CHUNKS, 10)),
            pltpu.SemaphoreType.DMA((CHUNKS, 10)),
        ],
        compiler_params=pltpu.CompilerParams(
            collective_id=0, has_side_effects=True, vmem_limit_bytes=48 * 1024 * 1024
        ),
        name="two_layers",
    )(*operands)


def solution(mesh):
    return jax.shard_map(
        shards,
        mesh=mesh,
        in_specs=(P("row", "col", None), P(), P(), P(), P(), P(), P(), P()),
        out_specs=P("row", "col", None),
        check_vma=False,
    )
```

```python
import jax
import jax.numpy as jnp
from jax import lax
from jax.experimental import pallas as pl
from jax.experimental.pallas import tpu as pltpu
from jax.sharding import PartitionSpec as P

F32, BF16 = jnp.float32, jnp.bfloat16
MESH = pl.DeviceIdType.MESH
D = 128
FF = 384
ROWS, COLS = 24, 32
STEP = 8
TRIPS = ROWS // STEP
WIDE = 24
ROWS_OF = ((3, 11, 19, 4, 12, 20), (9, 17, 10, 18, 1, 2), (5, 13, 6, 14, 21, 22), (7, 15, 8, 16, 23, 0))
EDGE = (0, 1, 2, 21, 22, 23)
GROUPS = ((3, 4), (11, 12), (19, 20), (9, 10), (17, 18), (5, 6), (13, 14), (7, 8), (15, 16))
EDGE_GROUPS = ((1, 2), (21, 22), (23,), (0,))
CHUNKS = 4
PER = STEP // CHUNKS
TOK = PER * TRIPS * COLS
SIDE = PER * TRIPS * WIDE
BLOCK = TRIPS * (COLS + 2 * WIDE)
LOG2E = 1.4426950408889634


def pieces_of(j):
    inner = [i for i in ROWS_OF[j] if i not in EDGE]
    outer = [i for i in ROWS_OF[j] if i in EDGE]
    return [(0, inner)] + ([(len(inner), outer)] if outer else [])


def segments(rows):
    return [[(i, a, b) for i in rows] for a, b in ((24, 32), (8, 24), (0, 8))]


def place_in(j, segs, per_row):
    found = {}
    for first, rows in pieces_of(j):
        at = first * per_row
        for seg in segs:
            a, b = seg
            for i in rows:
                found[i, a] = at
                at += b - a
    return found


def lanes_and_rows(rows, lanes):
    at = lax.broadcasted_iota(jnp.int32, (rows, 1), 0)
    return at >> 5, at & 31, lax.broadcasted_iota(jnp.int32, (1, lanes), 1)


def as_mask(ok):
    return jnp.where(ok, 1.0, 0.0).astype(BF16)


def row_mask(first, rows, queries=2):
    a, c, n = lanes_and_rows(queries * COLS, rows * COLS)
    step = (n >> 5) + first - a
    return as_mask((step >= 0) & (step <= 6) & (abs((n & 31) - c) <= 3))


def side_mask(first, queries=2):
    a, c, n = lanes_and_rows(queries * COLS, 64)
    step = 2 * (n >> 4) + ((n >> 2) & 1) + first - a
    at = (n & 3) + jnp.where((n & 8) == 0, -4, COLS)
    return as_mask((step >= 0) & (step <= 6) & (abs(at - c) <= 3))


def far_mask():
    t, c, n = lanes_and_rows(TRIPS * COLS, 3 * BLOCK)
    first = (n >= BLOCK).astype(jnp.int32)
    second = (n >= 2 * BLOCK).astype(jnp.int32)
    n = n - BLOCK * (first + second)
    left, right = TRIPS * COLS, TRIPS * (COLS + WIDE)
    m = jnp.where(n >= right, n - right, n - left)
    t2 = (m >= WIDE).astype(jnp.int32) + (m >= 2 * WIDE).astype(jnp.int32)
    m = m - WIDE * t2 + jnp.where(n >= right, COLS, -WIDE)
    key_col = jnp.where(n < left, n & 31, m)
    key_row = TRIPS * (2 * second - first) + jnp.where(n < left, n >> 5, t2)
    step = key_col - c
    return as_mask(
        (abs(key_row - t) <= 3) & ((step & (STEP - 1)) == 0) & (abs(step) <= 3 * STEP)
    )


def dot(a, b):
    return jnp.dot(a, b, preferred_element_type=F32)


def dot_nt(a, b):
    return lax.dot_general(a, b, (((1,), (1,)), ((), ())), preferred_element_type=F32)


def norm(x, gain):
    return x * lax.rsqrt(jnp.mean(x * x, axis=-1, keepdims=True) + 1e-6) * gain


def unit(x, ones):
    return x * lax.rsqrt(dot((x * x).astype(BF16), ones) + 1e-6)


OPERANDS = 8


def kernel(*refs):
    body(refs[:OPERANDS], *refs[OPERANDS:])


def body(
    given, out,
    tok, again, wqkv, sscale, wout, mgain, win, wdown, s_given, mown, mside, mfar,
    k0, v0, k0e, v0e, k0s, v0s, q0, acc0, x2, upx, dnx, pack_l, pack_r, beside,
    h1, rc, lr, q1, k1, v1, acc1, s_near, r_near, s_far, r_far,
):
    row, col = lax.axis_index("row"), lax.axis_index("col")
    n_row, n_col = lax.axis_size("row"), lax.axis_size("col")
    up, down = lax.rem(row + n_row - 1, n_row), lax.rem(row + 1, n_row)
    left, right = lax.rem(col + n_col - 1, n_col), lax.rem(col + 1, n_col)

    own = (tok, again, wqkv, sscale, wout, mgain, win, wdown)
    fetches = [
        pltpu.make_async_copy(src, dst, s_given.at[i])
        for i, (src, dst) in enumerate(zip(given, own))
    ]
    for fetch in fetches:
        fetch.start()

    barrier = pltpu.get_barrier_semaphore()
    exists = {"up": row > 0, "down": row < n_row - 1, "left": col > 0, "right": col < n_col - 1}
    device_at = {"up": (up, col), "down": (down, col), "left": (row, left), "right": (row, right)}
    opposite = {"up": "down", "down": "up", "left": "right", "right": "left"}

    absent = {
        "up": (upx, beside.at[:, pl.ds(0, 16)], rc.at[0], lr.at[1]),
        "down": (dnx, beside.at[:, pl.ds(112, 16)], rc.at[1], lr.at[2]),
        "left": (beside.at[0, pl.ds(16, 96)], lr.at[0, :, 0]),
        "right": (beside.at[1, pl.ds(16, 96)], lr.at[0, :, 1]),
    }
    for way, refs in absent.items():

        @pl.when(jnp.logical_not(exists[way]))
        def _(refs=refs):
            for ref in refs:
                ref[...] = jnp.zeros(ref.shape, ref.dtype)

    for way, device in device_at.items():

        @pl.when(exists[way])
        def _(device=device):
            pl.semaphore_signal(barrier, inc=1, device_id=device, device_id_type=MESH)

    has_up, has_down, has_left, has_right = (exists[way].astype(F32) for way in device_at)
    greeted = sum(exists[way].astype(jnp.int32) for way in device_at)
    row_ok = (jnp.float32(1), has_up, has_down)

    mown[...] = row_mask(0, 8)
    mside[...] = side_mask(0)
    mfar[...] = far_mask()

    fetches[0].wait()
    x0 = tok[...].astype(F32)
    even, odd = (x0.reshape(ROWS // 2, 2, COLS, D)[:, i] for i in range(2))
    slot = lax.broadcasted_iota(jnp.int32, (1, 8, 1), 1) < 4
    pack_l[...] = (
        jnp.where(slot, even[:, :8], pltpu.roll(odd[:, :8], 4, 1)).reshape(96, D).astype(BF16)
    )
    pack_r[...] = (
        jnp.where(slot, pltpu.roll(even[:, COLS - 8 :], 4, 1), odd[:, COLS - 8 :])
        .reshape(96, D)
        .astype(BF16)
    )

    class Message:
        def __init__(self, src, dst, sems, at, way):
            self.copy = pltpu.make_async_remote_copy(
                src_ref=src, dst_ref=dst, send_sem=sems[0].at[at], recv_sem=sems[1].at[at],
                device_id=device_at[way], device_id_type=MESH,
            )
            self.sends, self.receives = exists[way], exists[opposite[way]]
            pl.when(self.sends)(self.copy.start)

        def wait_recv(self):
            pl.when(self.receives)(self.copy.wait_recv)

        def wait_send(self):
            pl.when(self.sends)(self.copy.wait_send)

    send = Message

    lane = lax.broadcasted_iota(jnp.int32, (1, 2 * D), 1)
    first_head = (lane & (D // 2)) == 0
    low = jnp.where(first_head[:, :D], 1.0, 0.0)
    high = 1.0 - low
    same = (lax.broadcasted_iota(jnp.int32, (D, D), 0) < D // 2) == (
        lax.broadcasted_iota(jnp.int32, (D, D), 1) < D // 2
    )
    ones = jnp.where(same, 1.0, 0.0).astype(BF16)

    def query_scale(layer):
        scale = sscale[layer : layer + 1]
        return (scale[:, :1] * low + scale[:, 1:] * high) * LOG2E

    for fetch in fetches[1:]:
        fetch.wait()

    def attend(query, parts):
        size = query.shape[0] // 2
        total = None
        for key, value, mask in parts:
            weight = jnp.exp2(dot_nt(query, key)).astype(BF16)
            weight = weight.reshape(2, size, -1) * mask[None]
            part = dot(weight.reshape(2 * size, -1), value)
            total = part if total is None else total + part
        return jnp.where(first_head, total[:size], total[size:])

    qkv = dot(norm(x0.reshape(ROWS * COLS, D), again[0:1]).astype(BF16), wqkv[0])
    q = unit(qkv[:, :D], ones) * query_scale(0)
    q0[0] = (q * low).astype(BF16)
    q0[1] = (q * high).astype(BF16)
    k0[...] = unit(qkv[:, D : 2 * D], ones).astype(BF16)
    v0[:, :D] = qkv[:, 2 * D :].astype(BF16)
    v0[:, D:] = jnp.ones((ROWS * COLS, D), BF16)

    pl.semaphore_wait(barrier, greeted)
    near = (s_near, r_near)
    near_copies = [
        send(pack_r, beside.at[0, pl.ds(16, 96)], near, 0, "right"),
        send(pack_l, beside.at[1, pl.ds(16, 96)], near, 1, "left"),
        send(given[0].at[pl.ds(ROWS - 3, 3)], upx, near, 2, "down"),
        send(given[0].at[pl.ds(0, 3)], dnx, near, 3, "up"),
    ]

    def query_of(rows):
        size = len(rows) * COLS
        return q0[:, pl.ds(rows[0] * COLS, size)].reshape(2 * size, D)

    def finish(x, attended, layer):
        x1 = x + dot(attended.astype(BF16), wout[layer])
        inner = dot(norm(x1, mgain[layer : layer + 1]).astype(BF16), win[layer])
        value, gate = inner[:, :FF], inner[:, FF:]
        half = 0.5 * gate * value
        hidden = half + half * jnp.tanh(
            gate * (0.7978845608028654 + (0.7978845608028654 * 0.044715) * (gate * gate))
        )
        return x1 + dot(hidden.astype(BF16), wdown[layer])

    sides = [[] for _ in range(CHUNKS)]
    centres = [[] for _ in range(CHUNKS)]
    relays = [[] for _ in range(CHUNKS)]

    def first_layer(parts, attended):
        tokens = [(i, a, b) for _, _, part in parts for i, a, b in part]
        x = jnp.concatenate([tok[i].astype(F32)[a:b] for i, a, b in tokens], axis=0)
        x = finish(x, jnp.concatenate([attended(i)[a:b] for i, a, b in tokens], axis=0), 0)
        h = norm(x, again[1:2]).astype(BF16)
        at = 0
        for j, start, part in parts:
            size = sum(b - a for _, a, b in part)
            h1[j, pl.ds(start, size)] = h[at : at + size]
            x2[j, pl.ds(start, size)] = x[at : at + size]
            at += size

    def to_side(j, which, at, size, to):
        side, way = (0, "right") if which < 3 else (1, "left")
        sems = (s_far.at[j], r_far.at[j])
        src, part = h1.at[j, pl.ds(at, size)], pl.ds(to, size)
        sides[j].append(send(src, lr.at[0, j, side, part], sems, which, way))

    def to_rows(j, k, at, size):
        sems = (s_far.at[j], r_far.at[j])
        part = pl.ds(at, size)
        centres[j].extend(
            [
                send(h1.at[j, part], rc.at[0, j, part], sems, k, "down"),
                send(h1.at[j, part], rc.at[1, j, part], sems, k + 1, "up"),
            ]
        )

    def own_result(i):
        result = acc0[pl.ds(i * COLS, COLS)]
        return result[:, :D] / result[:, D:]

    def side_results(all_groups):
        attended = {}
        for rows in all_groups:
            i = rows[0]
            first = 2 * ((i + 1) // 2) - 4
            keys = pl.ds((i + 1) // 2 * 16, 64)
            whole = len(rows) == 2
            mask = mside[...] if whole else side_mask(first - i + 3, 1)
            parts = [(k0s[keys], v0s[keys], mask)]
            if i < 3:
                parts.append((k0e[pl.ds(0, 96)], v0e[pl.ds(0, 96)], row_mask(-i, 3, len(rows))))
            if rows[-1] + 4 > ROWS:
                mask = row_mask(ROWS + 3 - i, 3, len(rows))
                parts.append((k0e[pl.ds(96, 96)], v0e[pl.ds(96, 96)], mask))
            result = acc0[pl.ds(i * COLS, len(rows) * COLS)] + attend(query_of(rows), parts)
            result = result[:, :D] / result[:, D:]
            for at, one in enumerate(rows):
                attended[one] = result[at * COLS : (at + 1) * COLS]
        return attended

    def inner_columns():
        inner = [(j, pieces_of(j)[0][1]) for j in range(CHUNKS)]
        first_layer([(j, len(rows) * 8, segments(rows)[1]) for j, rows in inner], own_result)
        for j, rows in inner:
            n = len(rows)
            to_side(j, 0, n * 8, n * 16, n * 8)
            to_side(j, 3, n * 8, n * 16, 0)

    def outer_columns():
        inner = [(j, pieces_of(j)[0][1]) for j in range(CHUNKS)]
        attended = side_results(GROUPS)
        parts = []
        for j, rows in inner:
            segs = segments(rows)
            parts += [(j, 0, segs[0]), (j, len(rows) * 24, segs[2])]
        first_layer(parts, attended.get)
        for j, rows in inner:
            n = len(rows)
            to_side(j, 1, 0, n * 8, 0)
            to_side(j, 4, n * 24, n * 8, n * 16)
        for j, rows in inner:
            to_rows(j, 6, 0, len(rows) * COLS)

    def edge_rows():
        outer = [(j, *pieces_of(j)[1]) for j in range(1, CHUNKS)]
        attended = side_results(EDGE_GROUPS)
        first_layer(
            [(j, first * COLS, sum(segments(rows), [])) for j, first, rows in outer], attended.get
        )
        for j, first, rows in outer:
            n = len(rows)
            to_side(j, 2, first * COLS, n * WIDE, first * WIDE)
            to_side(j, 5, first * COLS + n * 8, n * WIDE, first * WIDE)
        for j, first, rows in outer:
            to_rows(j, 8, first * COLS, len(rows) * COLS)

    for rows in GROUPS + EDGE_GROUPS:
        i, end = rows[0], min(rows[-1] + 4, ROWS)
        begin = max(i - 3, 0)
        keys = pl.ds(begin * COLS, (end - begin) * COLS)
        whole = end - begin == 8
        mask = mown[...] if whole else row_mask(begin - i + 3, end - begin, len(rows))
        acc0[pl.ds(i * COLS, len(rows) * COLS)] = attend(
            query_of(rows), [(k0[keys], v0[keys], mask)]
        )
    inner_columns()
    v0e[pl.ds(0, 96), D:] = jnp.full((96, D), has_up).astype(BF16)
    v0e[pl.ds(96, 96), D:] = jnp.full((96, D), has_down).astype(BF16)
    for d in range(3):
        flags = jnp.concatenate(
            [
                jnp.full((TRIPS * COLS, D), row_ok[d]),
                jnp.full((TRIPS * WIDE, D), row_ok[d] * has_left),
                jnp.full((TRIPS * WIDE, D), row_ok[d] * has_right),
            ],
            axis=0,
        ).astype(BF16)
        for r in range(STEP):
            v1[r, pl.ds(d * BLOCK, BLOCK), D:] = flags

    def halo_keys(x):
        kv = dot(norm(x, again[0:1]).astype(BF16), wqkv[0, :, D:])
        return unit(kv[:, :D], ones).astype(BF16), kv[:, D:]

    def side_tokens(at, size):
        both = [beside[i, pl.ds(at, size)].astype(F32).reshape(size // 8, 8, D) for i in range(2)]
        return jnp.stack(both, axis=1).reshape(2 * size, D)

    def side_ok(size, flag):
        at = lax.broadcasted_iota(jnp.int32, (size, D), 0)
        return jnp.where((at & 8) == 0, has_left, has_right) * flag

    for copy in near_copies[:2]:
        copy.wait_recv()
    near_copies += [
        send(beside.at[:, pl.ds(96, 16)], beside.at[:, pl.ds(0, 16)], near, 4, "down"),
        send(beside.at[:, pl.ds(16, 16)], beside.at[:, pl.ds(112, 16)], near, 5, "up"),
    ]
    key, value = halo_keys(side_tokens(16, 96))
    k0s[pl.ds(32, 192)] = key
    ok = side_ok(192, 1.0)
    v0s[pl.ds(32, 192), :D] = (value * ok).astype(BF16)
    v0s[pl.ds(32, 192), D:] = ok.astype(BF16)

    def far_halo():
        for copy in near_copies[2:]:
            copy.wait_recv()
        x = jnp.concatenate(
            [
                upx[...].astype(F32).reshape(96, D),
                dnx[...].astype(F32).reshape(96, D),
                side_tokens(0, 16),
                side_tokens(112, 16),
            ],
            axis=0,
        )
        key, value = halo_keys(x)
        k0e[...] = key[:192]
        v0e[pl.ds(0, 96), :D] = (value[:96] * has_up).astype(BF16)
        v0e[pl.ds(96, 96), :D] = (value[96:192] * has_down).astype(BF16)
        for at, place, flag in ((192, 0, has_up), (224, 224, has_down)):
            ok = side_ok(32, flag)
            k0s[pl.ds(place, 32)] = key[at : at + 32]
            v0s[pl.ds(place, 32), :D] = (value[at : at + 32] * ok).astype(BF16)
            v0s[pl.ds(place, 32), D:] = ok.astype(BF16)

    def relay(j, k):
        for copy in sides[j][4 * k : 4 + 4 * k]:
            copy.wait_recv()
        sems = (s_far.at[j], r_far.at[j])
        first, rows = pieces_of(j)[k]
        part = pl.ds(first * WIDE, len(rows) * WIDE)
        relays[j] += [
            send(lr.at[0, j, :, part], lr.at[1, j, :, part], sems, 10 + 2 * k, "down"),
            send(lr.at[0, j, :, part], lr.at[2, j, :, part], sems, 11 + 2 * k, "up"),
        ]

    def residues(j):
        firsts = sorted({i % STEP for i in ROWS_OF[j]})
        return [[i + STEP * t for t in range(TRIPS)] for i in firsts]

    def whole_rows(array, j, rows):
        where = place_in(j, ((24, 32), (8, 24), (0, 8)), COLS)
        return [
            array[where[i, a] : where[i, a] + b - a]
            for i in rows
            for a, b in ((0, 8), (8, 24), (24, 32))
        ]

    def far_keys(j, d):
        centre = h1[j] if d == 0 else rc[d - 1, j]
        kv = dot(jnp.concatenate([centre, lr[d, j].reshape(2 * SIDE, D)], axis=0), wqkv[1, :, D:])
        key, value = unit(kv[:, :D], ones), kv[:, D:]
        value = jnp.concatenate(
            [
                value[:TOK] * row_ok[d],
                value[TOK : TOK + SIDE] * (row_ok[d] * has_left),
                value[TOK + SIDE :] * (row_ok[d] * has_right),
            ],
            axis=0,
        )
        on_left = place_in(j, ((24, 32), (8, 24)), WIDE)
        on_right = place_in(j, ((8, 24), (0, 8)), WIDE)
        beside_of = (
            (TOK, on_left, ((8, 24), (24, 32))),
            (TOK + SIDE, on_right, ((0, 8), (8, 24))),
        )
        for r, rows in enumerate(residues(j)):
            for array, ref, lanes in ((key, k1, slice(None)), (value, v1, slice(0, D))):
                piece = jnp.concatenate(
                    whole_rows(array, j, rows)
                    + [
                        array[base + at[i, a] : base + at[i, a] + b - a]
                        for base, at, order in beside_of
                        for i in rows
                        for a, b in order
                    ],
                    axis=0,
                )
                ref[PER * j + r, pl.ds(d * BLOCK, BLOCK), lanes] = piece.astype(BF16)

    def far_own(j):
        q = unit(dot(h1[j], wqkv[1, :, :D]), ones) * query_scale(1)
        far_keys(j, 0)
        for r, rows in enumerate(residues(j)):
            part = jnp.concatenate(whole_rows(q, j, rows), axis=0)
            query = jnp.concatenate([part * low, part * high], axis=0).astype(BF16)
            q1[PER * j + r] = query
            keys = (PER * j + r, pl.ds(0, BLOCK))
            acc1[PER * j + r] = attend(query, [(k1[keys], v1[keys], mfar[:, :BLOCK])])

    def far_layer(j):
        for copy in centres[j] + relays[j]:
            copy.wait_recv()
        far_keys(j, 1)
        far_keys(j, 2)
        attended = {}
        for r, rows in enumerate(residues(j)):
            keys = (PER * j + r, pl.ds(BLOCK, 2 * BLOCK))
            result = acc1[PER * j + r] + attend(
                q1[PER * j + r], [(k1[keys], v1[keys], mfar[:, BLOCK:])]
            )
            result = result[:, :D] / result[:, D:]
            for t, i in enumerate(rows):
                attended[i] = result[t * COLS : (t + 1) * COLS]
        order = [t for _, rows in pieces_of(j) for seg in segments(rows) for t in seg]
        x = finish(x2[j], jnp.concatenate([attended[i][a:b] for i, a, b in order], axis=0), 1)
        for i in ROWS_OF[j]:
            out[i] = jnp.concatenate(whole_rows(x, j, [i]), axis=0).astype(BF16)

    outer_columns()
    far_halo()
    edge_rows()
    for j in range(CHUNKS):
        relay(j, 0)
    far_own(0)
    for j in range(1, CHUNKS):
        relay(j, 1)
    far_layer(0)
    for j in range(1, CHUNKS):
        far_own(j)
    for j in range(1, CHUNKS):
        far_layer(j)
    for copy in near_copies + sum(sides + centres + relays, []):
        copy.wait_send()


def shards(tokens, attn_gain, w_qkv, score_scale, w_out, mlp_gain, w_in, down_weight):
    operands = (tokens, attn_gain, w_qkv, score_scale, w_out, mlp_gain, w_in, down_weight)
    operands = [pltpu.with_memory_space_constraint(a, pltpu.HBM) for a in operands]
    return pl.pallas_call(
        kernel,
        out_shape=jax.ShapeDtypeStruct((ROWS, COLS, D), BF16),
        in_specs=[pl.BlockSpec(memory_space=pltpu.HBM)] * OPERANDS,
        out_specs=pl.BlockSpec(memory_space=pltpu.VMEM),
        scratch_shapes=[pltpu.VMEM(a.shape, a.dtype) for a in operands]
        + [
            pltpu.SemaphoreType.DMA((OPERANDS,)),
            pltpu.VMEM((64, 256), BF16),
            pltpu.VMEM((64, 64), BF16),
            pltpu.VMEM((TRIPS * COLS, 3 * BLOCK), BF16),
            pltpu.VMEM((ROWS * COLS, D), BF16),
            pltpu.VMEM((ROWS * COLS, 2 * D), BF16),
            pltpu.VMEM((192, D), BF16),
            pltpu.VMEM((192, 2 * D), BF16),
            pltpu.VMEM((256, D), BF16),
            pltpu.VMEM((256, 2 * D), BF16),
            pltpu.VMEM((2, ROWS * COLS, D), BF16),
            pltpu.VMEM((ROWS * COLS, 2 * D), F32),
            pltpu.VMEM((CHUNKS, TOK, D), F32),
            pltpu.VMEM((3, COLS, D), BF16),
            pltpu.VMEM((3, COLS, D), BF16),
            pltpu.VMEM((96, D), BF16),
            pltpu.VMEM((96, D), BF16),
            pltpu.VMEM((2, 128, D), BF16),
            pltpu.VMEM((CHUNKS, TOK, D), BF16),
            pltpu.VMEM((2, CHUNKS, TOK, D), BF16),
            pltpu.VMEM((3, CHUNKS, 2, SIDE, D), BF16),
            pltpu.VMEM((STEP, 2 * TRIPS * COLS, D), BF16),
            pltpu.VMEM((STEP, 3 * BLOCK, D), BF16),
            pltpu.VMEM((STEP, 3 * BLOCK, 2 * D), BF16),
            pltpu.VMEM((STEP, TRIPS * COLS, 2 * D), F32),
            pltpu.SemaphoreType.DMA((6,)),
            pltpu.SemaphoreType.DMA((6,)),
            pltpu.SemaphoreType.DMA((CHUNKS, 14)),
            pltpu.SemaphoreType.DMA((CHUNKS, 14)),
        ],
        compiler_params=pltpu.CompilerParams(
            collective_id=0, has_side_effects=True, vmem_limit_bytes=48 * 1024 * 1024
        ),
        name="two_layers",
    )(*operands)


def solution(mesh):
    return jax.shard_map(
        shards,
        mesh=mesh,
        in_specs=(P("row", "col", None), P(), P(), P(), P(), P(), P(), P()),
        out_specs=P("row", "col", None),
        check_vma=False,
    )
```

```python
import jax
import jax.numpy as jnp
from jax import lax
from jax.experimental import pallas as pl
from jax.experimental.pallas import tpu as pltpu
from jax.sharding import PartitionSpec as P

F32, BF16 = jnp.float32, jnp.bfloat16
MESH = pl.DeviceIdType.MESH
D = 128
FF = 384
ROWS, COLS = 24, 32
STEP = 8
TRIPS = ROWS // STEP
WIDE = 24
ROWS_OF = ((3, 11, 19, 4, 12, 20), (9, 17, 10, 18, 1, 2), (5, 13, 6, 14, 21, 22), (7, 15, 8, 16, 23, 0))
EDGE = (0, 1, 2, 21, 22, 23)
GROUPS = ((3, 4), (11, 12), (19, 20), (9, 10), (17, 18), (5, 6), (13, 14), (7, 8), (15, 16))
EDGE_GROUPS = ((1, 2), (21, 22), (23,), (0,))
CHUNKS = 4
PER = STEP // CHUNKS
TOK = PER * TRIPS * COLS
SIDE = PER * TRIPS * WIDE
BLOCK = TRIPS * (COLS + 2 * WIDE)
LOG2E = 1.4426950408889634


def pieces_of(j):
    inner = [i for i in ROWS_OF[j] if i not in EDGE]
    outer = [i for i in ROWS_OF[j] if i in EDGE]
    return [(0, inner)] + ([(len(inner), outer)] if outer else [])


def segments(rows):
    return [[(i, a, b) for i in rows] for a, b in ((24, 32), (8, 24), (0, 8))]


def place_in(j, segs, per_row):
    found = {}
    for first, rows in pieces_of(j):
        at = first * per_row
        for seg in segs:
            a, b = seg
            for i in rows:
                found[i, a] = at
                at += b - a
    return found


def lanes_and_rows(rows, lanes):
    at = lax.broadcasted_iota(jnp.int32, (rows, 1), 0)
    return at >> 5, at & 31, lax.broadcasted_iota(jnp.int32, (1, lanes), 1)


def as_mask(ok):
    return jnp.where(ok, 1.0, 0.0).astype(BF16)


def row_mask(first, rows, queries=2):
    a, c, n = lanes_and_rows(queries * COLS, rows * COLS)
    step = (n >> 5) + first - a
    return as_mask((step >= 0) & (step <= 6) & (abs((n & 31) - c) <= 3))


def side_mask(first, queries=2):
    a, c, n = lanes_and_rows(queries * COLS, 64)
    step = 2 * (n >> 4) + ((n >> 2) & 1) + first - a
    at = (n & 3) + jnp.where((n & 8) == 0, -4, COLS)
    return as_mask((step >= 0) & (step <= 6) & (abs(at - c) <= 3))


def far_mask():
    t, c, n = lanes_and_rows(TRIPS * COLS, 3 * BLOCK)
    first = (n >= BLOCK).astype(jnp.int32)
    second = (n >= 2 * BLOCK).astype(jnp.int32)
    n = n - BLOCK * (first + second)
    left, right = TRIPS * COLS, TRIPS * (COLS + WIDE)
    m = jnp.where(n >= right, n - right, n - left)
    t2 = (m >= WIDE).astype(jnp.int32) + (m >= 2 * WIDE).astype(jnp.int32)
    m = m - WIDE * t2 + jnp.where(n >= right, COLS, -WIDE)
    key_col = jnp.where(n < left, n & 31, m)
    key_row = TRIPS * (2 * second - first) + jnp.where(n < left, n >> 5, t2)
    step = key_col - c
    return as_mask(
        (abs(key_row - t) <= 3) & ((step & (STEP - 1)) == 0) & (abs(step) <= 3 * STEP)
    )


def dot(a, b):
    return jnp.dot(a, b, preferred_element_type=F32)


def dot_nt(a, b):
    return lax.dot_general(a, b, (((1,), (1,)), ((), ())), preferred_element_type=F32)


def norm(x, gain):
    return x * lax.rsqrt(jnp.mean(x * x, axis=-1, keepdims=True) + 1e-6) * gain


def unit(x):
    first = lax.broadcasted_iota(jnp.int32, (1, D), 1) < D // 2
    square = x * x
    low = jnp.sum(jnp.where(first, square, 0.0), axis=-1, keepdims=True)
    high = jnp.sum(jnp.where(first, 0.0, square), axis=-1, keepdims=True)
    return x * jnp.where(first, lax.rsqrt(low + 1e-6), lax.rsqrt(high + 1e-6))


OPERANDS = 8


def kernel(*refs):
    body(refs[:OPERANDS], *refs[OPERANDS:])


def body(
    given, out,
    tok, again, wqkv, sscale, wout, mgain, win, wdown, s_given, mown, mside, mfar,
    k0, v0, k0e, v0e, k0s, v0s, q0, acc0, x2, upx, dnx, pack_l, pack_r, beside,
    h1, rc, lr, q1, k1, v1, acc1, s_near, r_near, s_far, r_far,
):
    row, col = lax.axis_index("row"), lax.axis_index("col")
    n_row, n_col = lax.axis_size("row"), lax.axis_size("col")
    up, down = lax.rem(row + n_row - 1, n_row), lax.rem(row + 1, n_row)
    left, right = lax.rem(col + n_col - 1, n_col), lax.rem(col + 1, n_col)

    own = (tok, again, wqkv, sscale, wout, mgain, win, wdown)
    fetches = [
        pltpu.make_async_copy(src, dst, s_given.at[i])
        for i, (src, dst) in enumerate(zip(given, own))
    ]
    for fetch in fetches:
        fetch.start()

    barrier = pltpu.get_barrier_semaphore()
    exists = {"up": row > 0, "down": row < n_row - 1, "left": col > 0, "right": col < n_col - 1}
    device_at = {"up": (up, col), "down": (down, col), "left": (row, left), "right": (row, right)}
    opposite = {"up": "down", "down": "up", "left": "right", "right": "left"}

    absent = {
        "up": (upx, beside.at[:, pl.ds(0, 16)], rc.at[0], lr.at[1]),
        "down": (dnx, beside.at[:, pl.ds(112, 16)], rc.at[1], lr.at[2]),
        "left": (beside.at[0, pl.ds(16, 96)], lr.at[0, :, 0]),
        "right": (beside.at[1, pl.ds(16, 96)], lr.at[0, :, 1]),
    }
    for way, refs in absent.items():

        @pl.when(jnp.logical_not(exists[way]))
        def _(refs=refs):
            for ref in refs:
                ref[...] = jnp.zeros(ref.shape, ref.dtype)

    for way, device in device_at.items():

        @pl.when(exists[way])
        def _(device=device):
            pl.semaphore_signal(barrier, inc=1, device_id=device, device_id_type=MESH)

    has_up, has_down, has_left, has_right = (exists[way].astype(F32) for way in device_at)
    greeted = sum(exists[way].astype(jnp.int32) for way in device_at)
    row_ok = (jnp.float32(1), has_up, has_down)

    mown[...] = row_mask(0, 8)
    mside[...] = side_mask(0)
    mfar[...] = far_mask()

    fetches[0].wait()
    x0 = tok[...].astype(F32)
    even, odd = (x0.reshape(ROWS // 2, 2, COLS, D)[:, i] for i in range(2))
    slot = lax.broadcasted_iota(jnp.int32, (1, 8, 1), 1) < 4
    pack_l[...] = (
        jnp.where(slot, even[:, :8], pltpu.roll(odd[:, :8], 4, 1)).reshape(96, D).astype(BF16)
    )
    pack_r[...] = (
        jnp.where(slot, pltpu.roll(even[:, COLS - 8 :], 4, 1), odd[:, COLS - 8 :])
        .reshape(96, D)
        .astype(BF16)
    )

    def send(src, dst, sems, at, way):
        copy = pltpu.make_async_remote_copy(
            src_ref=src, dst_ref=dst, send_sem=sems[0].at[at], recv_sem=sems[1].at[at],
            device_id=device_at[way], device_id_type=MESH,
        )
        return way, copy

    def each(copies, act, receiving=False):
        for way in ("right", "left", "down", "up"):
            mine = [copy for to, copy in copies if to == way]
            if mine:

                @pl.when(exists[opposite[way] if receiving else way])
                def _(mine=mine):
                    for copy in mine:
                        act(copy)

    def start(copies):
        each(copies, lambda copy: copy.start())
        return copies

    def received(copies):
        each(copies, lambda copy: copy.wait_recv(), receiving=True)

    lane = lax.broadcasted_iota(jnp.int32, (1, 2 * D), 1)
    first_head = (lane & (D // 2)) == 0
    low = jnp.where(first_head[:, :D], 1.0, 0.0)
    high = 1.0 - low
    def query_scale(layer):
        scale = sscale[layer : layer + 1]
        return (scale[:, :1] * low + scale[:, 1:] * high) * LOG2E

    for fetch in fetches[1:]:
        fetch.wait()

    def attend(query, parts):
        size = query.shape[0] // 2
        total = None
        for key, value, mask in parts:
            weight = jnp.exp2(dot_nt(query, key)).astype(BF16)
            weight = weight.reshape(2, size, -1) * mask[None]
            part = dot(weight.reshape(2 * size, -1), value)
            total = part if total is None else total + part
        return jnp.where(first_head, total[:size], total[size:])

    qkv = dot(norm(x0.reshape(ROWS * COLS, D), again[0:1]).astype(BF16), wqkv[0])
    q = unit(qkv[:, :D]) * query_scale(0)
    q0[0] = (q * low).astype(BF16)
    q0[1] = (q * high).astype(BF16)
    k0[...] = unit(qkv[:, D : 2 * D]).astype(BF16)
    v0[:, :D] = qkv[:, 2 * D :].astype(BF16)
    v0[:, D:] = jnp.ones((ROWS * COLS, D), BF16)

    pl.semaphore_wait(barrier, greeted)
    near = (s_near, r_near)
    near_copies = start([
        send(pack_r, beside.at[0, pl.ds(16, 96)], near, 0, "right"),
        send(pack_l, beside.at[1, pl.ds(16, 96)], near, 1, "left"),
        send(given[0].at[pl.ds(ROWS - 3, 3)], upx, near, 2, "down"),
        send(given[0].at[pl.ds(0, 3)], dnx, near, 3, "up"),
    ])

    def query_of(rows):
        size = len(rows) * COLS
        return q0[:, pl.ds(rows[0] * COLS, size)].reshape(2 * size, D)

    def finish(x, attended, layer):
        x1 = x + dot(attended.astype(BF16), wout[layer])
        inner = dot(norm(x1, mgain[layer : layer + 1]).astype(BF16), win[layer])
        value, gate = inner[:, :FF], inner[:, FF:]
        half = 0.5 * gate * value
        hidden = half + half * jnp.tanh(
            gate * (0.7978845608028654 + (0.7978845608028654 * 0.044715) * (gate * gate))
        )
        return x1 + dot(hidden.astype(BF16), wdown[layer])

    sides = [[] for _ in range(CHUNKS)]
    centres = [[] for _ in range(CHUNKS)]
    relays = [[] for _ in range(CHUNKS)]

    def first_layer(parts, attended):
        tokens = [(i, a, b) for _, _, part in parts for i, a, b in part]
        x = jnp.concatenate([tok[i].astype(F32)[a:b] for i, a, b in tokens], axis=0)
        x = finish(x, jnp.concatenate([attended(i)[a:b] for i, a, b in tokens], axis=0), 0)
        h = norm(x, again[1:2]).astype(BF16)
        at = 0
        for j, start, part in parts:
            size = sum(b - a for _, a, b in part)
            h1[j, pl.ds(start, size)] = h[at : at + size]
            x2[j, pl.ds(start, size)] = x[at : at + size]
            at += size

    begun = []

    def fresh():
        new = [c for c in sum(sides + centres + relays, []) if not any(c is b for b in begun)]
        begun.extend(new)
        return new

    def to_side(j, which, at, size, to):
        side, way = (0, "right") if which < 3 else (1, "left")
        sems = (s_far.at[j], r_far.at[j])
        src, part = h1.at[j, pl.ds(at, size)], pl.ds(to, size)
        sides[j].append(send(src, lr.at[0, j, side, part], sems, which, way))

    def to_rows(j, k, at, size):
        sems = (s_far.at[j], r_far.at[j])
        part = pl.ds(at, size)
        centres[j].extend(
            [
                send(h1.at[j, part], rc.at[0, j, part], sems, k, "down"),
                send(h1.at[j, part], rc.at[1, j, part], sems, k + 1, "up"),
            ]
        )

    def own_result(i):
        result = acc0[pl.ds(i * COLS, COLS)]
        return result[:, :D] / result[:, D:]

    def side_results(all_groups):
        attended = {}
        for rows in all_groups:
            i = rows[0]
            first = 2 * ((i + 1) // 2) - 4
            keys = pl.ds((i + 1) // 2 * 16, 64)
            whole = len(rows) == 2
            mask = mside[...] if whole else side_mask(first - i + 3, 1)
            parts = [(k0s[keys], v0s[keys], mask)]
            if i < 3:
                parts.append((k0e[pl.ds(0, 96)], v0e[pl.ds(0, 96)], row_mask(-i, 3, len(rows))))
            if rows[-1] + 4 > ROWS:
                mask = row_mask(ROWS + 3 - i, 3, len(rows))
                parts.append((k0e[pl.ds(96, 96)], v0e[pl.ds(96, 96)], mask))
            result = acc0[pl.ds(i * COLS, len(rows) * COLS)] + attend(query_of(rows), parts)
            result = result[:, :D] / result[:, D:]
            for at, one in enumerate(rows):
                attended[one] = result[at * COLS : (at + 1) * COLS]
        return attended

    def inner_columns():
        inner = [(j, pieces_of(j)[0][1]) for j in range(CHUNKS)]
        first_layer([(j, len(rows) * 8, segments(rows)[1]) for j, rows in inner], own_result)
        for j, rows in inner:
            n = len(rows)
            to_side(j, 0, n * 8, n * 16, n * 8)
            to_side(j, 3, n * 8, n * 16, 0)
        start(fresh())

    def outer_columns():
        inner = [(j, pieces_of(j)[0][1]) for j in range(CHUNKS)]
        attended = side_results(GROUPS)
        parts = []
        for j, rows in inner:
            segs = segments(rows)
            parts += [(j, 0, segs[0]), (j, len(rows) * 24, segs[2])]
        first_layer(parts, attended.get)
        for j, rows in inner:
            n = len(rows)
            to_side(j, 1, 0, n * 8, 0)
            to_side(j, 4, n * 24, n * 8, n * 16)
        for j, rows in inner:
            to_rows(j, 6, 0, len(rows) * COLS)
        start(fresh())

    def edge_rows():
        outer = [(j, *pieces_of(j)[1]) for j in range(1, CHUNKS)]
        attended = side_results(EDGE_GROUPS)
        first_layer(
            [(j, first * COLS, sum(segments(rows), [])) for j, first, rows in outer], attended.get
        )
        for j, first, rows in outer:
            n = len(rows)
            to_side(j, 2, first * COLS, n * WIDE, first * WIDE)
            to_side(j, 5, first * COLS + n * 8, n * WIDE, first * WIDE)
        for j, first, rows in outer:
            to_rows(j, 8, first * COLS, len(rows) * COLS)
        start(fresh())

    for rows in GROUPS + EDGE_GROUPS:
        i, end = rows[0], min(rows[-1] + 4, ROWS)
        begin = max(i - 3, 0)
        keys = pl.ds(begin * COLS, (end - begin) * COLS)
        whole = end - begin == 8
        mask = mown[...] if whole else row_mask(begin - i + 3, end - begin, len(rows))
        acc0[pl.ds(i * COLS, len(rows) * COLS)] = attend(
            query_of(rows), [(k0[keys], v0[keys], mask)]
        )
    inner_columns()
    v0e[pl.ds(0, 96), D:] = jnp.full((96, D), has_up).astype(BF16)
    v0e[pl.ds(96, 96), D:] = jnp.full((96, D), has_down).astype(BF16)
    for d in range(3):
        flags = jnp.concatenate(
            [
                jnp.full((TRIPS * COLS, D), row_ok[d]),
                jnp.full((TRIPS * WIDE, D), row_ok[d] * has_left),
                jnp.full((TRIPS * WIDE, D), row_ok[d] * has_right),
            ],
            axis=0,
        ).astype(BF16)
        for r in range(STEP):
            v1[r, pl.ds(d * BLOCK, BLOCK), D:] = flags

    def halo_keys(x):
        kv = dot(norm(x, again[0:1]).astype(BF16), wqkv[0, :, D:])
        return unit(kv[:, :D]).astype(BF16), kv[:, D:]

    def side_tokens(at, size):
        both = [beside[i, pl.ds(at, size)].astype(F32).reshape(size // 8, 8, D) for i in range(2)]
        return jnp.stack(both, axis=1).reshape(2 * size, D)

    def side_ok(size, flag):
        at = lax.broadcasted_iota(jnp.int32, (size, D), 0)
        return jnp.where((at & 8) == 0, has_left, has_right) * flag

    received(near_copies[:2])
    near_copies += start([
        send(beside.at[:, pl.ds(96, 16)], beside.at[:, pl.ds(0, 16)], near, 4, "down"),
        send(beside.at[:, pl.ds(16, 16)], beside.at[:, pl.ds(112, 16)], near, 5, "up"),
    ])
    key, value = halo_keys(side_tokens(16, 96))
    k0s[pl.ds(32, 192)] = key
    ok = side_ok(192, 1.0)
    v0s[pl.ds(32, 192), :D] = value.astype(BF16)
    v0s[pl.ds(32, 192), D:] = ok.astype(BF16)

    def far_halo():
        received(near_copies[2:])
        x = jnp.concatenate(
            [
                upx[...].astype(F32).reshape(96, D),
                dnx[...].astype(F32).reshape(96, D),
                side_tokens(0, 16),
                side_tokens(112, 16),
            ],
            axis=0,
        )
        key, value = halo_keys(x)
        k0e[...] = key[:192]
        v0e[pl.ds(0, 96), :D] = value[:96].astype(BF16)
        v0e[pl.ds(96, 96), :D] = value[96:192].astype(BF16)
        for at, place, flag in ((192, 0, has_up), (224, 224, has_down)):
            ok = side_ok(32, flag)
            k0s[pl.ds(place, 32)] = key[at : at + 32]
            v0s[pl.ds(place, 32), :D] = value[at : at + 32].astype(BF16)
            v0s[pl.ds(place, 32), D:] = ok.astype(BF16)

    def relay(chunks, k):
        received(sum([sides[j][4 * k : 4 + 4 * k] for j in chunks], []))
        for j in chunks:
            sems = (s_far.at[j], r_far.at[j])
            first, rows = pieces_of(j)[k]
            part = pl.ds(first * WIDE, len(rows) * WIDE)
            relays[j] += [
                send(lr.at[0, j, :, part], lr.at[1, j, :, part], sems, 10 + 2 * k, "down"),
                send(lr.at[0, j, :, part], lr.at[2, j, :, part], sems, 11 + 2 * k, "up"),
            ]
        start(fresh())

    def residues(j):
        firsts = sorted({i % STEP for i in ROWS_OF[j]})
        return [[i + STEP * t for t in range(TRIPS)] for i in firsts]

    def whole_rows(array, j, rows):
        where = place_in(j, ((24, 32), (8, 24), (0, 8)), COLS)
        return [
            array[where[i, a] : where[i, a] + b - a]
            for i in rows
            for a, b in ((0, 8), (8, 24), (24, 32))
        ]

    def far_keys(j, d):
        centre = h1[j] if d == 0 else rc[d - 1, j]
        kv = dot(jnp.concatenate([centre, lr[d, j].reshape(2 * SIDE, D)], axis=0), wqkv[1, :, D:])
        key, value = unit(kv[:, :D]), kv[:, D:]
        on_left = place_in(j, ((24, 32), (8, 24)), WIDE)
        on_right = place_in(j, ((8, 24), (0, 8)), WIDE)
        beside_of = (
            (TOK, on_left, ((8, 24), (24, 32))),
            (TOK + SIDE, on_right, ((0, 8), (8, 24))),
        )
        for r, rows in enumerate(residues(j)):
            for array, ref, lanes in ((key, k1, slice(None)), (value, v1, slice(0, D))):
                piece = jnp.concatenate(
                    whole_rows(array, j, rows)
                    + [
                        array[base + at[i, a] : base + at[i, a] + b - a]
                        for base, at, order in beside_of
                        for i in rows
                        for a, b in order
                    ],
                    axis=0,
                )
                ref[PER * j + r, pl.ds(d * BLOCK, BLOCK), lanes] = piece.astype(BF16)

    def far_own(j):
        q = unit(dot(h1[j], wqkv[1, :, :D])) * query_scale(1)
        far_keys(j, 0)
        for r, rows in enumerate(residues(j)):
            part = jnp.concatenate(whole_rows(q, j, rows), axis=0)
            query = jnp.concatenate([part * low, part * high], axis=0).astype(BF16)
            q1[PER * j + r] = query
            keys = (PER * j + r, pl.ds(0, BLOCK))
            acc1[PER * j + r] = attend(query, [(k1[keys], v1[keys], mfar[:, :BLOCK])])

    def far_layer(j):
        far_keys(j, 1)
        far_keys(j, 2)
        attended = {}
        for r, rows in enumerate(residues(j)):
            keys = (PER * j + r, pl.ds(BLOCK, 2 * BLOCK))
            result = acc1[PER * j + r] + attend(
                q1[PER * j + r], [(k1[keys], v1[keys], mfar[:, BLOCK:])]
            )
            result = result[:, :D] / result[:, D:]
            for t, i in enumerate(rows):
                attended[i] = result[t * COLS : (t + 1) * COLS]
        order = [t for _, rows in pieces_of(j) for seg in segments(rows) for t in seg]
        x = finish(x2[j], jnp.concatenate([attended[i][a:b] for i, a, b in order], axis=0), 1)
        for i in ROWS_OF[j]:
            out[i] = jnp.concatenate(whole_rows(x, j, [i]), axis=0).astype(BF16)

    outer_columns()
    far_halo()
    edge_rows()
    last = range(1, CHUNKS)
    relay([0], 0)
    relay(last, 0)
    far_own(0)
    relay(last, 1)
    received(centres[0] + relays[0])
    far_layer(0)
    for j in last:
        far_own(j)
    received(sum([centres[j] + relays[j] for j in last], []))
    for j in last:
        far_layer(j)
    each(near_copies + sum(sides + centres + relays, []), lambda copy: copy.wait_send())


def shards(tokens, attn_gain, w_qkv, score_scale, w_out, mlp_gain, w_in, down_weight):
    operands = (tokens, attn_gain, w_qkv, score_scale, w_out, mlp_gain, w_in, down_weight)
    operands = [pltpu.with_memory_space_constraint(a, pltpu.HBM) for a in operands]
    return pl.pallas_call(
        kernel,
        out_shape=jax.ShapeDtypeStruct((ROWS, COLS, D), BF16),
        in_specs=[pl.BlockSpec(memory_space=pltpu.HBM)] * OPERANDS,
        out_specs=pl.BlockSpec(memory_space=pltpu.VMEM),
        scratch_shapes=[pltpu.VMEM(a.shape, a.dtype) for a in operands]
        + [
            pltpu.SemaphoreType.DMA((OPERANDS,)),
            pltpu.VMEM((64, 256), BF16),
            pltpu.VMEM((64, 64), BF16),
            pltpu.VMEM((TRIPS * COLS, 3 * BLOCK), BF16),
            pltpu.VMEM((ROWS * COLS, D), BF16),
            pltpu.VMEM((ROWS * COLS, 2 * D), BF16),
            pltpu.VMEM((192, D), BF16),
            pltpu.VMEM((192, 2 * D), BF16),
            pltpu.VMEM((256, D), BF16),
            pltpu.VMEM((256, 2 * D), BF16),
            pltpu.VMEM((2, ROWS * COLS, D), BF16),
            pltpu.VMEM((ROWS * COLS, 2 * D), F32),
            pltpu.VMEM((CHUNKS, TOK, D), F32),
            pltpu.VMEM((3, COLS, D), BF16),
            pltpu.VMEM((3, COLS, D), BF16),
            pltpu.VMEM((96, D), BF16),
            pltpu.VMEM((96, D), BF16),
            pltpu.VMEM((2, 128, D), BF16),
            pltpu.VMEM((CHUNKS, TOK, D), BF16),
            pltpu.VMEM((2, CHUNKS, TOK, D), BF16),
            pltpu.VMEM((3, CHUNKS, 2, SIDE, D), BF16),
            pltpu.VMEM((STEP, 2 * TRIPS * COLS, D), BF16),
            pltpu.VMEM((STEP, 3 * BLOCK, D), BF16),
            pltpu.VMEM((STEP, 3 * BLOCK, 2 * D), BF16),
            pltpu.VMEM((STEP, TRIPS * COLS, 2 * D), F32),
            pltpu.SemaphoreType.DMA((6,)),
            pltpu.SemaphoreType.DMA((6,)),
            pltpu.SemaphoreType.DMA((CHUNKS, 14)),
            pltpu.SemaphoreType.DMA((CHUNKS, 14)),
        ],
        compiler_params=pltpu.CompilerParams(
            collective_id=0, has_side_effects=True, vmem_limit_bytes=48 * 1024 * 1024
        ),
        name="two_layers",
    )(*operands)


def solution(mesh):
    return jax.shard_map(
        shards,
        mesh=mesh,
        in_specs=(P("row", "col", None), P(), P(), P(), P(), P(), P(), P()),
        out_specs=P("row", "col", None),
        check_vma=False,
    )
```

```python
import jax
import jax.numpy as jnp
from jax import lax
from jax.experimental import pallas as pl
from jax.experimental.pallas import tpu as pltpu
from jax.sharding import PartitionSpec as P

F32, BF16 = jnp.float32, jnp.bfloat16
MESH = pl.DeviceIdType.MESH
D = 128
FF = 384
ROWS, COLS = 24, 32
STEP = 8
TRIPS = ROWS // STEP
WIDE = 24
ROWS_OF = ((3, 11, 19, 4, 12, 20), (9, 17, 10, 18, 1, 2), (5, 13, 6, 14, 21, 22), (7, 15, 8, 16, 23, 0))
EDGE = (0, 1, 2, 21, 22, 23)
GROUPS = ((3, 4), (11, 12), (19, 20), (9, 10), (17, 18), (5, 6), (13, 14), (7, 8), (15, 16))
EDGE_GROUPS = ((1, 2), (21, 22), (23,), (0,))
CHUNKS = 4
PER = STEP // CHUNKS
TOK = PER * TRIPS * COLS
SIDE = PER * TRIPS * WIDE
BLOCK = TRIPS * (COLS + 2 * WIDE)
LOG2E = 1.4426950408889634


def pieces_of(j):
    inner = [i for i in ROWS_OF[j] if i not in EDGE]
    outer = [i for i in ROWS_OF[j] if i in EDGE]
    return [(0, inner)] + ([(len(inner), outer)] if outer else [])


def segments(rows):
    return [[(i, a, b) for i in rows] for a, b in ((24, 32), (8, 24), (0, 8))]


def place_in(j, segs, per_row):
    found = {}
    for first, rows in pieces_of(j):
        at = first * per_row
        for seg in segs:
            a, b = seg
            for i in rows:
                found[i, a] = at
                at += b - a
    return found


def lanes_and_rows(rows, lanes):
    at = lax.broadcasted_iota(jnp.int32, (rows, 1), 0)
    return at >> 5, at & 31, lax.broadcasted_iota(jnp.int32, (1, lanes), 1)


def as_mask(ok):
    return jnp.where(ok, 1.0, 0.0).astype(BF16)


def row_mask(first, rows, queries=2):
    a, c, n = lanes_and_rows(queries * COLS, rows * COLS)
    step = (n >> 5) + first - a
    return as_mask((step >= 0) & (step <= 6) & (abs((n & 31) - c) <= 3))


def side_mask(first, queries=2):
    a, c, n = lanes_and_rows(queries * COLS, 64)
    step = 2 * (n >> 4) + ((n >> 2) & 1) + first - a
    at = (n & 3) + jnp.where((n & 8) == 0, -4, COLS)
    return as_mask((step >= 0) & (step <= 6) & (abs(at - c) <= 3))


def far_mask():
    t, c, n = lanes_and_rows(TRIPS * COLS, 3 * BLOCK)
    first = (n >= BLOCK).astype(jnp.int32)
    second = (n >= 2 * BLOCK).astype(jnp.int32)
    n = n - BLOCK * (first + second)
    left, right = TRIPS * COLS, TRIPS * (COLS + WIDE)
    m = jnp.where(n >= right, n - right, n - left)
    t2 = (m >= WIDE).astype(jnp.int32) + (m >= 2 * WIDE).astype(jnp.int32)
    m = m - WIDE * t2 + jnp.where(n >= right, COLS, -WIDE)
    key_col = jnp.where(n < left, n & 31, m)
    key_row = TRIPS * (2 * second - first) + jnp.where(n < left, n >> 5, t2)
    step = key_col - c
    return as_mask(
        (abs(key_row - t) <= 3) & ((step & (STEP - 1)) == 0) & (abs(step) <= 3 * STEP)
    )


def dot(a, b):
    return jnp.dot(a, b, preferred_element_type=F32)


def dot_nt(a, b):
    return lax.dot_general(a, b, (((1,), (1,)), ((), ())), preferred_element_type=F32)


def norm(x, gain):
    return x * lax.rsqrt(jnp.mean(x * x, axis=-1, keepdims=True) + 1e-6) * gain


def unit(x):
    first = lax.broadcasted_iota(jnp.int32, (1, D), 1) < D // 2
    square = x * x
    low = jnp.sum(jnp.where(first, square, 0.0), axis=-1, keepdims=True)
    high = jnp.sum(jnp.where(first, 0.0, square), axis=-1, keepdims=True)
    return x * jnp.where(first, lax.rsqrt(low + 1e-6), lax.rsqrt(high + 1e-6))


OPERANDS = 8


def kernel(*refs):
    body(refs[:OPERANDS], *refs[OPERANDS:])


def body(
    given, out,
    tok, again, wqkv, sscale, wout, mgain, win, wdown, s_given, mown, mside, mfar,
    k0, v0, k0e, v0e, k0s, v0s, q0, acc0, x2, upx, dnx, pack_l, pack_r, beside,
    h1, rc, lr, q1, k1, v1, acc1, s_near, r_near, s_far, r_far,
):
    row, col = lax.axis_index("row"), lax.axis_index("col")
    n_row, n_col = lax.axis_size("row"), lax.axis_size("col")
    up, down = lax.rem(row + n_row - 1, n_row), lax.rem(row + 1, n_row)
    left, right = lax.rem(col + n_col - 1, n_col), lax.rem(col + 1, n_col)

    own = (tok, again, wqkv, sscale, wout, mgain, win, wdown)
    fetches = [
        pltpu.make_async_copy(src, dst, s_given.at[i])
        for i, (src, dst) in enumerate(zip(given, own))
    ]
    for fetch in fetches:
        fetch.start()

    barrier = pltpu.get_barrier_semaphore()
    exists = {"up": row > 0, "down": row < n_row - 1, "left": col > 0, "right": col < n_col - 1}
    device_at = {"up": (up, col), "down": (down, col), "left": (row, left), "right": (row, right)}
    opposite = {"up": "down", "down": "up", "left": "right", "right": "left"}

    absent = {
        "up": (upx, beside.at[:, pl.ds(0, 16)], rc.at[0], lr.at[1]),
        "down": (dnx, beside.at[:, pl.ds(112, 16)], rc.at[1], lr.at[2]),
        "left": (beside.at[0, pl.ds(16, 96)], lr.at[0, :, 0]),
        "right": (beside.at[1, pl.ds(16, 96)], lr.at[0, :, 1]),
    }
    for way, refs in absent.items():

        @pl.when(jnp.logical_not(exists[way]))
        def _(refs=refs):
            for ref in refs:
                ref[...] = jnp.zeros(ref.shape, ref.dtype)

    for way, device in device_at.items():

        @pl.when(exists[way])
        def _(device=device):
            pl.semaphore_signal(barrier, inc=1, device_id=device, device_id_type=MESH)

    has_up, has_down, has_left, has_right = (exists[way].astype(F32) for way in device_at)
    greeted = sum(exists[way].astype(jnp.int32) for way in device_at)
    row_ok = (jnp.float32(1), has_up, has_down)

    mown[...] = row_mask(0, 8)
    mside[...] = side_mask(0)
    mfar[...] = far_mask()

    fetches[0].wait()
    x0 = tok[...].astype(F32)
    even, odd = (x0.reshape(ROWS // 2, 2, COLS, D)[:, i] for i in range(2))
    slot = lax.broadcasted_iota(jnp.int32, (1, 8, 1), 1) < 4
    pack_l[...] = (
        jnp.where(slot, even[:, :8], pltpu.roll(odd[:, :8], 4, 1)).reshape(96, D).astype(BF16)
    )
    pack_r[...] = (
        jnp.where(slot, pltpu.roll(even[:, COLS - 8 :], 4, 1), odd[:, COLS - 8 :])
        .reshape(96, D)
        .astype(BF16)
    )

    def send(src, dst, sems, at, way):
        copy = pltpu.make_async_remote_copy(
            src_ref=src, dst_ref=dst, send_sem=sems[0].at[at], recv_sem=sems[1].at[at],
            device_id=device_at[way], device_id_type=MESH,
        )
        return way, copy

    def each(copies, act, receiving=False):
        for way in ("right", "left", "down", "up"):
            mine = [copy for to, copy in copies if to == way]
            if mine:

                @pl.when(exists[opposite[way] if receiving else way])
                def _(mine=mine):
                    for copy in mine:
                        act(copy)

    def start(copies):
        each(copies, lambda copy: copy.start())
        return copies

    def received(copies):
        each(copies, lambda copy: copy.wait_recv(), receiving=True)

    lane = lax.broadcasted_iota(jnp.int32, (1, 2 * D), 1)
    first_head = (lane & (D // 2)) == 0
    low = jnp.where(first_head[:, :D], 1.0, 0.0)
    high = 1.0 - low
    def query_scale(layer):
        scale = sscale[layer : layer + 1]
        return (scale[:, :1] * low + scale[:, 1:] * high) * LOG2E

    for fetch in fetches[1:]:
        fetch.wait()

    def attend(query, parts):
        size = query.shape[0] // 2
        total = None
        for key, value, mask in parts:
            weight = jnp.exp2(dot_nt(query, key)).astype(BF16)
            weight = weight.reshape(2, size, -1) * mask[None]
            part = dot(weight.reshape(2 * size, -1), value)
            total = part if total is None else total + part
        return jnp.where(first_head, total[:size], total[size:])

    qkv = dot(norm(x0.reshape(ROWS * COLS, D), again[0:1]).astype(BF16), wqkv[0])
    q = unit(qkv[:, :D]) * query_scale(0)
    q0[0] = (q * low).astype(BF16)
    q0[1] = (q * high).astype(BF16)
    k0[...] = unit(qkv[:, D : 2 * D]).astype(BF16)
    v0[:, :D] = qkv[:, 2 * D :].astype(BF16)
    v0[:, D:] = jnp.ones((ROWS * COLS, D), BF16)

    pl.semaphore_wait(barrier, greeted)
    near = (s_near, r_near)
    near_copies = start([
        send(pack_r, beside.at[0, pl.ds(16, 96)], near, 0, "right"),
        send(pack_l, beside.at[1, pl.ds(16, 96)], near, 1, "left"),
        send(given[0].at[pl.ds(ROWS - 3, 3)], upx, near, 2, "down"),
        send(given[0].at[pl.ds(0, 3)], dnx, near, 3, "up"),
    ])

    def query_of(rows):
        size = len(rows) * COLS
        return q0[:, pl.ds(rows[0] * COLS, size)].reshape(2 * size, D)

    def finish(x, attended, layer):
        x1 = x + dot(attended.astype(BF16), wout[layer])
        inner = dot(norm(x1, mgain[layer : layer + 1]).astype(BF16), win[layer])
        value, gate = inner[:, :FF], inner[:, FF:]
        half = 0.5 * gate * value
        hidden = half + half * jnp.tanh(
            gate * (0.7978845608028654 + (0.7978845608028654 * 0.044715) * (gate * gate))
        )
        return x1 + dot(hidden.astype(BF16), wdown[layer])

    sides = [[] for _ in range(CHUNKS)]
    centres = [[] for _ in range(CHUNKS)]
    relays = [[] for _ in range(CHUNKS)]

    def first_layer(parts, attended):
        tokens = [(i, a, b) for _, _, part in parts for i, a, b in part]
        x = jnp.concatenate([tok[i].astype(F32)[a:b] for i, a, b in tokens], axis=0)
        x = finish(x, jnp.concatenate([attended(i)[a:b] for i, a, b in tokens], axis=0), 0)
        h = norm(x, again[1:2]).astype(BF16)
        at = 0
        for j, start, part in parts:
            size = sum(b - a for _, a, b in part)
            h1[j, pl.ds(start, size)] = h[at : at + size]
            x2[j, pl.ds(start, size)] = x[at : at + size]
            at += size

    begun = []

    def fresh():
        new = [c for c in sum(sides + centres + relays, []) if not any(c is b for b in begun)]
        begun.extend(new)
        return new

    def to_side(j, which, at, size, to):
        side, way = (0, "right") if which < 3 else (1, "left")
        sems = (s_far.at[j], r_far.at[j])
        src, part = h1.at[j, pl.ds(at, size)], pl.ds(to, size)
        sides[j].append(send(src, lr.at[0, j, side, part], sems, which, way))

    def to_rows(j, k, at, size):
        sems = (s_far.at[j], r_far.at[j])
        part = pl.ds(at, size)
        centres[j].extend(
            [
                send(h1.at[j, part], rc.at[0, j, part], sems, k, "down"),
                send(h1.at[j, part], rc.at[1, j, part], sems, k + 1, "up"),
            ]
        )

    def own_result(i):
        result = acc0[pl.ds(i * COLS, COLS)]
        return result[:, :D] / result[:, D:]

    def side_results(all_groups):
        attended = {}
        for rows in all_groups:
            i = rows[0]
            first = 2 * ((i + 1) // 2) - 4
            keys = pl.ds((i + 1) // 2 * 16, 64)
            whole = len(rows) == 2
            mask = mside[...] if whole else side_mask(first - i + 3, 1)
            parts = [(k0s[keys], v0s[keys], mask)]
            if i < 3:
                parts.append((k0e[pl.ds(0, 96)], v0e[pl.ds(0, 96)], row_mask(-i, 3, len(rows))))
            if rows[-1] + 4 > ROWS:
                mask = row_mask(ROWS + 3 - i, 3, len(rows))
                parts.append((k0e[pl.ds(96, 96)], v0e[pl.ds(96, 96)], mask))
            result = acc0[pl.ds(i * COLS, len(rows) * COLS)] + attend(query_of(rows), parts)
            result = result[:, :D] / result[:, D:]
            for at, one in enumerate(rows):
                attended[one] = result[at * COLS : (at + 1) * COLS]
        return attended

    def inner_columns():
        inner = [(j, pieces_of(j)[0][1]) for j in range(CHUNKS)]
        first_layer([(j, len(rows) * 8, segments(rows)[1]) for j, rows in inner], own_result)
        for j, rows in inner:
            n = len(rows)
            to_side(j, 0, n * 8, n * 16, n * 8)
            to_side(j, 3, n * 8, n * 16, 0)
        start(fresh())

    def outer_columns():
        inner = [(j, pieces_of(j)[0][1]) for j in range(CHUNKS)]
        attended = side_results(GROUPS)
        parts = []
        for j, rows in inner:
            segs = segments(rows)
            parts += [(j, 0, segs[0]), (j, len(rows) * 24, segs[2])]
        first_layer(parts, attended.get)
        for j, rows in inner:
            n = len(rows)
            to_side(j, 1, 0, n * 8, 0)
            to_side(j, 4, n * 24, n * 8, n * 16)
        for j, rows in inner:
            to_rows(j, 6, 0, len(rows) * COLS)
        start(fresh())

    def edge_rows():
        outer = [(j, *pieces_of(j)[1]) for j in range(1, CHUNKS)]
        attended = side_results(EDGE_GROUPS)
        first_layer(
            [(j, first * COLS, sum(segments(rows), [])) for j, first, rows in outer], attended.get
        )
        for j, first, rows in outer:
            n = len(rows)
            to_side(j, 2, first * COLS, n * WIDE, first * WIDE)
            to_side(j, 5, first * COLS + n * 8, n * WIDE, first * WIDE)
        for j, first, rows in outer:
            to_rows(j, 8, first * COLS, len(rows) * COLS)
        start(fresh())

    for rows in GROUPS + EDGE_GROUPS:
        i, end = rows[0], min(rows[-1] + 4, ROWS)
        begin = max(i - 3, 0)
        keys = pl.ds(begin * COLS, (end - begin) * COLS)
        whole = end - begin == 8
        mask = mown[...] if whole else row_mask(begin - i + 3, end - begin, len(rows))
        acc0[pl.ds(i * COLS, len(rows) * COLS)] = attend(
            query_of(rows), [(k0[keys], v0[keys], mask)]
        )
    inner_columns()
    v0e[pl.ds(0, 96), D:] = jnp.full((96, D), has_up).astype(BF16)
    v0e[pl.ds(96, 96), D:] = jnp.full((96, D), has_down).astype(BF16)
    for d in range(3):
        flags = jnp.concatenate(
            [
                jnp.full((TRIPS * COLS, D), row_ok[d]),
                jnp.full((TRIPS * WIDE, D), row_ok[d] * has_left),
                jnp.full((TRIPS * WIDE, D), row_ok[d] * has_right),
            ],
            axis=0,
        ).astype(BF16)
        for r in range(STEP):
            v1[r, pl.ds(d * BLOCK, BLOCK), D:] = flags

    def halo_keys(x):
        kv = dot(norm(x, again[0:1]).astype(BF16), wqkv[0, :, D:])
        return unit(kv[:, :D]).astype(BF16), kv[:, D:]

    def side_tokens(at, size):
        both = [beside[i, pl.ds(at, size)].astype(F32).reshape(size // 8, 8, D) for i in range(2)]
        return jnp.stack(both, axis=1).reshape(2 * size, D)

    def side_ok(size, flag):
        at = lax.broadcasted_iota(jnp.int32, (size, D), 0)
        return jnp.where((at & 8) == 0, has_left, has_right) * flag

    received(near_copies[:2])
    near_copies += start([
        send(beside.at[:, pl.ds(96, 16)], beside.at[:, pl.ds(0, 16)], near, 4, "down"),
        send(beside.at[:, pl.ds(16, 16)], beside.at[:, pl.ds(112, 16)], near, 5, "up"),
    ])
    key, value = halo_keys(side_tokens(16, 96))
    k0s[pl.ds(32, 192)] = key
    ok = side_ok(192, 1.0)
    v0s[pl.ds(32, 192), :D] = value.astype(BF16)
    v0s[pl.ds(32, 192), D:] = ok.astype(BF16)

    def far_halo():
        received(near_copies[2:])
        x = jnp.concatenate(
            [
                upx[...].astype(F32).reshape(96, D),
                dnx[...].astype(F32).reshape(96, D),
                side_tokens(0, 16),
                side_tokens(112, 16),
            ],
            axis=0,
        )
        key, value = halo_keys(x)
        k0e[...] = key[:192]
        v0e[pl.ds(0, 96), :D] = value[:96].astype(BF16)
        v0e[pl.ds(96, 96), :D] = value[96:192].astype(BF16)
        for at, place, flag in ((192, 0, has_up), (224, 224, has_down)):
            ok = side_ok(32, flag)
            k0s[pl.ds(place, 32)] = key[at : at + 32]
            v0s[pl.ds(place, 32), :D] = value[at : at + 32].astype(BF16)
            v0s[pl.ds(place, 32), D:] = ok.astype(BF16)

    def relay(chunks, k):
        received(sum([sides[j][4 * k : 4 + 4 * k] for j in chunks], []))
        for j in chunks:
            sems = (s_far.at[j], r_far.at[j])
            first, rows = pieces_of(j)[k]
            part = pl.ds(first * WIDE, len(rows) * WIDE)
            relays[j] += [
                send(lr.at[0, j, :, part], lr.at[1, j, :, part], sems, 10 + 2 * k, "down"),
                send(lr.at[0, j, :, part], lr.at[2, j, :, part], sems, 11 + 2 * k, "up"),
            ]
        start(fresh())

    def residues(j):
        firsts = sorted({i % STEP for i in ROWS_OF[j]})
        return [[i + STEP * t for t in range(TRIPS)] for i in firsts]

    def whole_rows(array, j, rows):
        where = place_in(j, ((24, 32), (8, 24), (0, 8)), COLS)
        return [
            array[where[i, a] : where[i, a] + b - a]
            for i in rows
            for a, b in ((0, 8), (8, 24), (24, 32))
        ]

    def far_keys(wanted):
        tokens = []
        for j, d in wanted:
            tokens += [h1[j] if d == 0 else rc[d - 1, j], lr[d, j].reshape(2 * SIDE, D)]
        kv = dot(jnp.concatenate(tokens, axis=0), wqkv[1, :, D:])
        keys, values = unit(kv[:, :D]), kv[:, D:]
        for at, (j, d) in enumerate(wanted):
            part = slice(at * (TOK + 2 * SIDE), (at + 1) * (TOK + 2 * SIDE))
            keep_keys(j, d, keys[part], values[part])

    def keep_keys(j, d, key, value):
        on_left = place_in(j, ((24, 32), (8, 24)), WIDE)
        on_right = place_in(j, ((8, 24), (0, 8)), WIDE)
        beside_of = (
            (TOK, on_left, ((8, 24), (24, 32))),
            (TOK + SIDE, on_right, ((0, 8), (8, 24))),
        )
        for r, rows in enumerate(residues(j)):
            for array, ref, lanes in ((key, k1, slice(None)), (value, v1, slice(0, D))):
                piece = jnp.concatenate(
                    whole_rows(array, j, rows)
                    + [
                        array[base + at[i, a] : base + at[i, a] + b - a]
                        for base, at, order in beside_of
                        for i in rows
                        for a, b in order
                    ],
                    axis=0,
                )
                ref[PER * j + r, pl.ds(d * BLOCK, BLOCK), lanes] = piece.astype(BF16)

    def far_own(chunks):
        q = unit(dot(jnp.concatenate([h1[j] for j in chunks], axis=0), wqkv[1, :, :D]))
        q = q * query_scale(1)
        far_keys([(j, 0) for j in chunks])
        for at, j in enumerate(chunks):
            for r, rows in enumerate(residues(j)):
                part = whole_rows(q[at * TOK : (at + 1) * TOK], j, rows)
                part = jnp.concatenate(part, axis=0)
                query = jnp.concatenate([part * low, part * high], axis=0).astype(BF16)
                q1[PER * j + r] = query
                keys = (PER * j + r, pl.ds(0, BLOCK))
                acc1[PER * j + r] = attend(query, [(k1[keys], v1[keys], mfar[:, :BLOCK])])

    def far_layer(chunks):
        attended = []
        far_keys([(j, d) for j in chunks for d in (1, 2)])
        for j in chunks:
            found = {}
            for r, rows in enumerate(residues(j)):
                keys = (PER * j + r, pl.ds(BLOCK, 2 * BLOCK))
                result = acc1[PER * j + r] + attend(
                    q1[PER * j + r], [(k1[keys], v1[keys], mfar[:, BLOCK:])]
                )
                result = result[:, :D] / result[:, D:]
                for t, i in enumerate(rows):
                    found[i] = result[t * COLS : (t + 1) * COLS]
            order = [t for _, rows in pieces_of(j) for seg in segments(rows) for t in seg]
            attended += [found[i][a:b] for i, a, b in order]
        x = jnp.concatenate([x2[j] for j in chunks], axis=0)
        x = finish(x, jnp.concatenate(attended, axis=0), 1)
        for at, j in enumerate(chunks):
            for i in ROWS_OF[j]:
                rows = whole_rows(x[at * TOK : (at + 1) * TOK], j, [i])
                out[i] = jnp.concatenate(rows, axis=0).astype(BF16)

    outer_columns()
    far_halo()
    edge_rows()
    last = range(1, CHUNKS)
    relay([0], 0)
    relay(last, 0)
    far_own([0])
    relay(last, 1)
    received(centres[0] + relays[0])
    far_layer([0])
    far_own(last)
    received(sum([centres[j] + relays[j] for j in last], []))
    far_layer(last)
    each(near_copies + sum(sides + centres + relays, []), lambda copy: copy.wait_send())


def shards(tokens, attn_gain, w_qkv, score_scale, w_out, mlp_gain, w_in, down_weight):
    operands = (tokens, attn_gain, w_qkv, score_scale, w_out, mlp_gain, w_in, down_weight)
    operands = [pltpu.with_memory_space_constraint(a, pltpu.HBM) for a in operands]
    return pl.pallas_call(
        kernel,
        out_shape=jax.ShapeDtypeStruct((ROWS, COLS, D), BF16),
        in_specs=[pl.BlockSpec(memory_space=pltpu.HBM)] * OPERANDS,
        out_specs=pl.BlockSpec(memory_space=pltpu.VMEM),
        scratch_shapes=[pltpu.VMEM(a.shape, a.dtype) for a in operands]
        + [
            pltpu.SemaphoreType.DMA((OPERANDS,)),
            pltpu.VMEM((64, 256), BF16),
            pltpu.VMEM((64, 64), BF16),
            pltpu.VMEM((TRIPS * COLS, 3 * BLOCK), BF16),
            pltpu.VMEM((ROWS * COLS, D), BF16),
            pltpu.VMEM((ROWS * COLS, 2 * D), BF16),
            pltpu.VMEM((192, D), BF16),
            pltpu.VMEM((192, 2 * D), BF16),
            pltpu.VMEM((256, D), BF16),
            pltpu.VMEM((256, 2 * D), BF16),
            pltpu.VMEM((2, ROWS * COLS, D), BF16),
            pltpu.VMEM((ROWS * COLS, 2 * D), F32),
            pltpu.VMEM((CHUNKS, TOK, D), F32),
            pltpu.VMEM((3, COLS, D), BF16),
            pltpu.VMEM((3, COLS, D), BF16),
            pltpu.VMEM((96, D), BF16),
            pltpu.VMEM((96, D), BF16),
            pltpu.VMEM((2, 128, D), BF16),
            pltpu.VMEM((CHUNKS, TOK, D), BF16),
            pltpu.VMEM((2, CHUNKS, TOK, D), BF16),
            pltpu.VMEM((3, CHUNKS, 2, SIDE, D), BF16),
            pltpu.VMEM((STEP, 2 * TRIPS * COLS, D), BF16),
            pltpu.VMEM((STEP, 3 * BLOCK, D), BF16),
            pltpu.VMEM((STEP, 3 * BLOCK, 2 * D), BF16),
            pltpu.VMEM((STEP, TRIPS * COLS, 2 * D), F32),
            pltpu.SemaphoreType.DMA((6,)),
            pltpu.SemaphoreType.DMA((6,)),
            pltpu.SemaphoreType.DMA((CHUNKS, 14)),
            pltpu.SemaphoreType.DMA((CHUNKS, 14)),
        ],
        compiler_params=pltpu.CompilerParams(
            collective_id=0, has_side_effects=True, vmem_limit_bytes=48 * 1024 * 1024
        ),
        name="two_layers",
    )(*operands)


def solution(mesh):
    return jax.shard_map(
        shards,
        mesh=mesh,
        in_specs=(P("row", "col", None), P(), P(), P(), P(), P(), P(), P()),
        out_specs=P("row", "col", None),
        check_vma=False,
    )
```

```python
import jax
import jax.numpy as jnp
from jax import lax
from jax.experimental import pallas as pl
from jax.experimental.pallas import tpu as pltpu
from jax.sharding import PartitionSpec as P

F32, BF16 = jnp.float32, jnp.bfloat16
MESH = pl.DeviceIdType.MESH
D = 128
FF = 384
ROWS, COLS = 24, 32
STEP = 8
TRIPS = ROWS // STEP
WIDE = 24
ROWS_OF = ((3, 11, 19, 4, 12, 20), (9, 17, 10, 18, 1, 2), (5, 13, 6, 14, 21, 22), (7, 15, 8, 16, 23, 0))
EDGE = (0, 1, 2, 21, 22, 23)
GROUPS = ((3, 4), (11, 12), (19, 20), (9, 10), (17, 18), (5, 6), (13, 14), (7, 8), (15, 16))
SIDE_GROUPS = ((3, 4, 5, 6), (7, 8, 9, 10), (11, 12, 13, 14), (15, 16, 17, 18), (19, 20))
EDGE_GROUPS = ((1, 2), (21, 22), (23,), (0,))
CHUNKS = 4
PER = STEP // CHUNKS
TOK = PER * TRIPS * COLS
SIDE = PER * TRIPS * WIDE
BLOCK = TRIPS * (COLS + 2 * WIDE)
LOG2E = 1.4426950408889634


def pieces_of(j):
    inner = [i for i in ROWS_OF[j] if i not in EDGE]
    outer = [i for i in ROWS_OF[j] if i in EDGE]
    return [(0, inner)] + ([(len(inner), outer)] if outer else [])


def segments(rows):
    return [[(i, a, b) for i in rows] for a, b in ((24, 32), (8, 24), (0, 8))]


def place_in(j, segs, per_row):
    found = {}
    for first, rows in pieces_of(j):
        at = first * per_row
        for seg in segs:
            a, b = seg
            for i in rows:
                found[i, a] = at
                at += b - a
    return found


def lanes_and_rows(rows, lanes):
    at = lax.broadcasted_iota(jnp.int32, (rows, 1), 0)
    return at >> 5, at & 31, lax.broadcasted_iota(jnp.int32, (1, lanes), 1)


def as_mask(ok):
    return jnp.where(ok, 1.0, 0.0).astype(BF16)


def row_mask(first, rows, queries=2):
    a, c, n = lanes_and_rows(queries * COLS, rows * COLS)
    step = (n >> 5) + first - a
    return as_mask((step >= 0) & (step <= 6) & (abs((n & 31) - c) <= 3))


def side_mask(first, queries=2):
    a, c, n = lanes_and_rows(queries * COLS, 80 if queries == 4 else 64)
    step = 2 * (n >> 4) + ((n >> 2) & 1) + first - a
    at = (n & 3) + jnp.where((n & 8) == 0, -4, COLS)
    return as_mask((step >= 0) & (step <= 6) & (abs(at - c) <= 3))


def far_mask():
    t, c, n = lanes_and_rows(TRIPS * COLS, 3 * BLOCK)
    first = (n >= BLOCK).astype(jnp.int32)
    second = (n >= 2 * BLOCK).astype(jnp.int32)
    n = n - BLOCK * (first + second)
    left, right = TRIPS * COLS, TRIPS * (COLS + WIDE)
    m = jnp.where(n >= right, n - right, n - left)
    t2 = (m >= WIDE).astype(jnp.int32) + (m >= 2 * WIDE).astype(jnp.int32)
    m = m - WIDE * t2 + jnp.where(n >= right, COLS, -WIDE)
    key_col = jnp.where(n < left, n & 31, m)
    key_row = TRIPS * (2 * second - first) + jnp.where(n < left, n >> 5, t2)
    step = key_col - c
    return as_mask(
        (abs(key_row - t) <= 3) & ((step & (STEP - 1)) == 0) & (abs(step) <= 3 * STEP)
    )


def dot(a, b):
    return jnp.dot(a, b, preferred_element_type=F32)


def dot_nt(a, b):
    return lax.dot_general(a, b, (((1,), (1,)), ((), ())), preferred_element_type=F32)


def norm(x, gain):
    return x * lax.rsqrt(jnp.mean(x * x, axis=-1, keepdims=True) + 1e-6) * gain


def unit(x):
    first = lax.broadcasted_iota(jnp.int32, (1, D), 1) < D // 2
    square = x * x
    low = jnp.sum(jnp.where(first, square, 0.0), axis=-1, keepdims=True)
    high = jnp.sum(jnp.where(first, 0.0, square), axis=-1, keepdims=True)
    return x * jnp.where(first, lax.rsqrt(low + 1e-6), lax.rsqrt(high + 1e-6))


OPERANDS = 8


def kernel(*refs):
    body(refs[:OPERANDS], *refs[OPERANDS:])


def body(
    given, out,
    tok, again, wqkv, sscale, wout, mgain, win, wdown, s_given, mown, mside, mside4, mfar,
    k0, v0, k0e, v0e, k0s, v0s, q0, acc0, x2, upx, dnx, pack_l, pack_r, beside,
    h1, rc, lr, q1, k1, v1, acc1, s_near, r_near, s_far, r_far,
):
    row, col = lax.axis_index("row"), lax.axis_index("col")
    n_row, n_col = lax.axis_size("row"), lax.axis_size("col")
    up, down = lax.rem(row + n_row - 1, n_row), lax.rem(row + 1, n_row)
    left, right = lax.rem(col + n_col - 1, n_col), lax.rem(col + 1, n_col)

    own = (tok, again, wqkv, sscale, wout, mgain, win, wdown)
    fetches = [
        pltpu.make_async_copy(src, dst, s_given.at[i])
        for i, (src, dst) in enumerate(zip(given, own))
    ]
    for fetch in fetches:
        fetch.start()

    barrier = pltpu.get_barrier_semaphore()
    exists = {"up": row > 0, "down": row < n_row - 1, "left": col > 0, "right": col < n_col - 1}
    device_at = {"up": (up, col), "down": (down, col), "left": (row, left), "right": (row, right)}
    opposite = {"up": "down", "down": "up", "left": "right", "right": "left"}

    absent = {
        "up": (upx, beside.at[:, pl.ds(0, 16)], rc.at[0], lr.at[1]),
        "down": (dnx, beside.at[:, pl.ds(112, 16)], rc.at[1], lr.at[2]),
        "left": (beside.at[0, pl.ds(16, 96)], lr.at[0, :, 0]),
        "right": (beside.at[1, pl.ds(16, 96)], lr.at[0, :, 1]),
    }
    for way, refs in absent.items():

        @pl.when(jnp.logical_not(exists[way]))
        def _(refs=refs):
            for ref in refs:
                ref[...] = jnp.zeros(ref.shape, ref.dtype)

    for way, device in device_at.items():

        @pl.when(exists[way])
        def _(device=device):
            pl.semaphore_signal(barrier, inc=1, device_id=device, device_id_type=MESH)

    has_up, has_down, has_left, has_right = (exists[way].astype(F32) for way in device_at)
    greeted = sum(exists[way].astype(jnp.int32) for way in device_at)
    row_ok = (jnp.float32(1), has_up, has_down)

    mown[...] = row_mask(0, 8)
    mside[...] = side_mask(0)
    mside4[...] = side_mask(0, 4)
    mfar[...] = far_mask()

    fetches[0].wait()
    x0 = tok[...].astype(F32)
    even, odd = (x0.reshape(ROWS // 2, 2, COLS, D)[:, i] for i in range(2))
    slot = lax.broadcasted_iota(jnp.int32, (1, 8, 1), 1) < 4
    pack_l[...] = (
        jnp.where(slot, even[:, :8], pltpu.roll(odd[:, :8], 4, 1)).reshape(96, D).astype(BF16)
    )
    pack_r[...] = (
        jnp.where(slot, pltpu.roll(even[:, COLS - 8 :], 4, 1), odd[:, COLS - 8 :])
        .reshape(96, D)
        .astype(BF16)
    )

    def send(src, dst, sems, at, way):
        copy = pltpu.make_async_remote_copy(
            src_ref=src, dst_ref=dst, send_sem=sems[0].at[at], recv_sem=sems[1].at[at],
            device_id=device_at[way], device_id_type=MESH,
        )
        return way, copy

    def each(copies, act, receiving=False):
        for way in ("right", "left", "down", "up"):
            mine = [copy for to, copy in copies if to == way]
            if mine:

                @pl.when(exists[opposite[way] if receiving else way])
                def _(mine=mine):
                    for copy in mine:
                        act(copy)

    def start(copies):
        each(copies, lambda copy: copy.start())
        return copies

    def received(copies):
        each(copies, lambda copy: copy.wait_recv(), receiving=True)

    lane = lax.broadcasted_iota(jnp.int32, (1, 2 * D), 1)
    first_head = (lane & (D // 2)) == 0
    low = jnp.where(first_head[:, :D], 1.0, 0.0)
    high = 1.0 - low
    def query_scale(layer):
        scale = sscale[layer : layer + 1]
        return (scale[:, :1] * low + scale[:, 1:] * high) * LOG2E

    for fetch in fetches[1:]:
        fetch.wait()

    def attend(query, parts):
        size = query.shape[0] // 2
        total = None
        for key, value, mask in parts:
            weight = jnp.exp2(dot_nt(query, key)).astype(BF16)
            weight = weight.reshape(2, size, -1) * mask[None]
            part = dot(weight.reshape(2 * size, -1), value)
            total = part if total is None else total + part
        return jnp.where(first_head, total[:size], total[size:])

    qkv = dot(norm(x0.reshape(ROWS * COLS, D), again[0:1]).astype(BF16), wqkv[0])
    q = unit(qkv[:, :D]) * query_scale(0)
    q0[0] = (q * low).astype(BF16)
    q0[1] = (q * high).astype(BF16)
    k0[...] = unit(qkv[:, D : 2 * D]).astype(BF16)
    v0[:, :D] = qkv[:, 2 * D :].astype(BF16)
    v0[:, D:] = jnp.ones((ROWS * COLS, D), BF16)

    pl.semaphore_wait(barrier, greeted)
    near = (s_near, r_near)
    near_copies = start([
        send(pack_r, beside.at[0, pl.ds(16, 96)], near, 0, "right"),
        send(pack_l, beside.at[1, pl.ds(16, 96)], near, 1, "left"),
        send(given[0].at[pl.ds(ROWS - 3, 3)], upx, near, 2, "down"),
        send(given[0].at[pl.ds(0, 3)], dnx, near, 3, "up"),
    ])

    def query_of(rows):
        size = len(rows) * COLS
        return q0[:, pl.ds(rows[0] * COLS, size)].reshape(2 * size, D)

    def finish(x, attended, layer):
        x1 = x + dot(attended.astype(BF16), wout[layer])
        inner = dot(norm(x1, mgain[layer : layer + 1]).astype(BF16), win[layer])
        value, gate = inner[:, :FF], inner[:, FF:]
        half = 0.5 * gate * value
        hidden = half + half * jnp.tanh(
            gate * (0.7978845608028654 + (0.7978845608028654 * 0.044715) * (gate * gate))
        )
        return x1 + dot(hidden.astype(BF16), wdown[layer])

    sides = [[] for _ in range(CHUNKS)]
    centres = [[] for _ in range(CHUNKS)]
    relays = [[] for _ in range(CHUNKS)]

    def first_layer(parts, attended):
        tokens = [(i, a, b) for _, _, part in parts for i, a, b in part]
        x = jnp.concatenate([tok[i].astype(F32)[a:b] for i, a, b in tokens], axis=0)
        x = finish(x, jnp.concatenate([attended(i)[a:b] for i, a, b in tokens], axis=0), 0)
        h = norm(x, again[1:2]).astype(BF16)
        at = 0
        for j, start, part in parts:
            size = sum(b - a for _, a, b in part)
            h1[j, pl.ds(start, size)] = h[at : at + size]
            x2[j, pl.ds(start, size)] = x[at : at + size]
            at += size

    begun = []

    def fresh():
        new = [c for c in sum(sides + centres + relays, []) if not any(c is b for b in begun)]
        begun.extend(new)
        return new

    def to_side(j, which, at, size, to):
        side, way = (0, "right") if which < 3 else (1, "left")
        sems = (s_far.at[j], r_far.at[j])
        src, part = h1.at[j, pl.ds(at, size)], pl.ds(to, size)
        sides[j].append(send(src, lr.at[0, j, side, part], sems, which, way))

    def to_rows(j, k, at, size):
        sems = (s_far.at[j], r_far.at[j])
        part = pl.ds(at, size)
        centres[j].extend(
            [
                send(h1.at[j, part], rc.at[0, j, part], sems, k, "down"),
                send(h1.at[j, part], rc.at[1, j, part], sems, k + 1, "up"),
            ]
        )

    def own_result(i):
        result = acc0[pl.ds(i * COLS, COLS)]
        return result[:, :D] / result[:, D:]

    def side_results(all_groups):
        attended = {}
        for rows in all_groups:
            i = rows[0]
            first = 2 * ((i + 1) // 2) - 4
            keys = pl.ds((i + 1) // 2 * 16, 80 if len(rows) == 4 else 64)
            if len(rows) == 1:
                mask = side_mask(first - i + 3, 1)
            else:
                mask = mside[...] if len(rows) == 2 else mside4[...]
            parts = [(k0s[keys], v0s[keys], mask)]
            if i < 3:
                parts.append((k0e[pl.ds(0, 96)], v0e[pl.ds(0, 96)], row_mask(-i, 3, len(rows))))
            if rows[-1] + 4 > ROWS:
                mask = row_mask(ROWS + 3 - i, 3, len(rows))
                parts.append((k0e[pl.ds(96, 96)], v0e[pl.ds(96, 96)], mask))
            result = acc0[pl.ds(i * COLS, len(rows) * COLS)] + attend(query_of(rows), parts)
            result = result[:, :D] / result[:, D:]
            for at, one in enumerate(rows):
                attended[one] = result[at * COLS : (at + 1) * COLS]
        return attended

    def inner_columns():
        inner = [(j, pieces_of(j)[0][1]) for j in range(CHUNKS)]
        first_layer([(j, len(rows) * 8, segments(rows)[1]) for j, rows in inner], own_result)
        for j, rows in inner:
            n = len(rows)
            to_side(j, 0, n * 8, n * 16, n * 8)
            to_side(j, 3, n * 8, n * 16, 0)
        start(fresh())

    def outer_columns():
        inner = [(j, pieces_of(j)[0][1]) for j in range(CHUNKS)]
        attended = side_results(SIDE_GROUPS)
        parts = []
        for j, rows in inner:
            segs = segments(rows)
            parts += [(j, 0, segs[0]), (j, len(rows) * 24, segs[2])]
        first_layer(parts, attended.get)
        for j, rows in inner:
            n = len(rows)
            to_side(j, 1, 0, n * 8, 0)
            to_side(j, 4, n * 24, n * 8, n * 16)
        for j, rows in inner:
            to_rows(j, 6, 0, len(rows) * COLS)
        start(fresh())

    def edge_rows():
        outer = [(j, *pieces_of(j)[1]) for j in range(1, CHUNKS)]
        attended = side_results(EDGE_GROUPS)
        first_layer(
            [(j, first * COLS, sum(segments(rows), [])) for j, first, rows in outer], attended.get
        )
        for j, first, rows in outer:
            n = len(rows)
            to_side(j, 2, first * COLS, n * WIDE, first * WIDE)
            to_side(j, 5, first * COLS + n * 8, n * WIDE, first * WIDE)
        for j, first, rows in outer:
            to_rows(j, 8, first * COLS, len(rows) * COLS)
        start(fresh())

    for rows in GROUPS + EDGE_GROUPS:
        i, end = rows[0], min(rows[-1] + 4, ROWS)
        begin = max(i - 3, 0)
        keys = pl.ds(begin * COLS, (end - begin) * COLS)
        whole = end - begin == 8
        mask = mown[...] if whole else row_mask(begin - i + 3, end - begin, len(rows))
        acc0[pl.ds(i * COLS, len(rows) * COLS)] = attend(
            query_of(rows), [(k0[keys], v0[keys], mask)]
        )
    inner_columns()
    v0e[pl.ds(0, 96), D:] = jnp.full((96, D), has_up).astype(BF16)
    v0e[pl.ds(96, 96), D:] = jnp.full((96, D), has_down).astype(BF16)
    for d in range(3):
        flags = jnp.concatenate(
            [
                jnp.full((TRIPS * COLS, D), row_ok[d]),
                jnp.full((TRIPS * WIDE, D), row_ok[d] * has_left),
                jnp.full((TRIPS * WIDE, D), row_ok[d] * has_right),
            ],
            axis=0,
        ).astype(BF16)
        for r in range(STEP):
            v1[r, pl.ds(d * BLOCK, BLOCK), D:] = flags

    def halo_keys(x):
        kv = dot(norm(x, again[0:1]).astype(BF16), wqkv[0, :, D:])
        return unit(kv[:, :D]).astype(BF16), kv[:, D:]

    def side_tokens(at, size):
        both = [beside[i, pl.ds(at, size)].astype(F32).reshape(size // 8, 8, D) for i in range(2)]
        return jnp.stack(both, axis=1).reshape(2 * size, D)

    def side_ok(size, flag):
        at = lax.broadcasted_iota(jnp.int32, (size, D), 0)
        return jnp.where((at & 8) == 0, has_left, has_right) * flag

    received(near_copies[:2])
    near_copies += start([
        send(beside.at[:, pl.ds(96, 16)], beside.at[:, pl.ds(0, 16)], near, 4, "down"),
        send(beside.at[:, pl.ds(16, 16)], beside.at[:, pl.ds(112, 16)], near, 5, "up"),
    ])
    key, value = halo_keys(side_tokens(16, 96))
    k0s[pl.ds(32, 192)] = key
    ok = side_ok(192, 1.0)
    v0s[pl.ds(32, 192), :D] = value.astype(BF16)
    v0s[pl.ds(32, 192), D:] = ok.astype(BF16)

    def far_halo():
        received(near_copies[2:])
        x = jnp.concatenate(
            [
                upx[...].astype(F32).reshape(96, D),
                dnx[...].astype(F32).reshape(96, D),
                side_tokens(0, 16),
                side_tokens(112, 16),
            ],
            axis=0,
        )
        key, value = halo_keys(x)
        k0e[...] = key[:192]
        v0e[pl.ds(0, 96), :D] = value[:96].astype(BF16)
        v0e[pl.ds(96, 96), :D] = value[96:192].astype(BF16)
        for at, place, flag in ((192, 0, has_up), (224, 224, has_down)):
            ok = side_ok(32, flag)
            k0s[pl.ds(place, 32)] = key[at : at + 32]
            v0s[pl.ds(place, 32), :D] = value[at : at + 32].astype(BF16)
            v0s[pl.ds(place, 32), D:] = ok.astype(BF16)

    def relay(chunks, k):
        received(sum([sides[j][4 * k : 4 + 4 * k] for j in chunks], []))
        for j in chunks:
            sems = (s_far.at[j], r_far.at[j])
            first, rows = pieces_of(j)[k]
            part = pl.ds(first * WIDE, len(rows) * WIDE)
            relays[j] += [
                send(lr.at[0, j, :, part], lr.at[1, j, :, part], sems, 10 + 2 * k, "down"),
                send(lr.at[0, j, :, part], lr.at[2, j, :, part], sems, 11 + 2 * k, "up"),
            ]
        start(fresh())

    def residues(j):
        firsts = sorted({i % STEP for i in ROWS_OF[j]})
        return [[i + STEP * t for t in range(TRIPS)] for i in firsts]

    def whole_rows(array, j, rows):
        where = place_in(j, ((24, 32), (8, 24), (0, 8)), COLS)
        return [
            array[where[i, a] : where[i, a] + b - a]
            for i in rows
            for a, b in ((0, 8), (8, 24), (24, 32))
        ]

    def far_keys(wanted):
        tokens = []
        for j, d in wanted:
            tokens += [h1[j] if d == 0 else rc[d - 1, j], lr[d, j].reshape(2 * SIDE, D)]
        kv = dot(jnp.concatenate(tokens, axis=0), wqkv[1, :, D:])
        keys, values = unit(kv[:, :D]), kv[:, D:]
        for at, (j, d) in enumerate(wanted):
            part = slice(at * (TOK + 2 * SIDE), (at + 1) * (TOK + 2 * SIDE))
            keep_keys(j, d, keys[part], values[part])

    def keep_keys(j, d, key, value):
        on_left = place_in(j, ((24, 32), (8, 24)), WIDE)
        on_right = place_in(j, ((8, 24), (0, 8)), WIDE)
        beside_of = (
            (TOK, on_left, ((8, 24), (24, 32))),
            (TOK + SIDE, on_right, ((0, 8), (8, 24))),
        )
        for r, rows in enumerate(residues(j)):
            for array, ref, lanes in ((key, k1, slice(None)), (value, v1, slice(0, D))):
                piece = jnp.concatenate(
                    whole_rows(array, j, rows)
                    + [
                        array[base + at[i, a] : base + at[i, a] + b - a]
                        for base, at, order in beside_of
                        for i in rows
                        for a, b in order
                    ],
                    axis=0,
                )
                ref[PER * j + r, pl.ds(d * BLOCK, BLOCK), lanes] = piece.astype(BF16)

    def far_own(chunks):
        q = unit(dot(jnp.concatenate([h1[j] for j in chunks], axis=0), wqkv[1, :, :D]))
        q = q * query_scale(1)
        far_keys([(j, 0) for j in chunks])
        for at, j in enumerate(chunks):
            for r, rows in enumerate(residues(j)):
                part = whole_rows(q[at * TOK : (at + 1) * TOK], j, rows)
                part = jnp.concatenate(part, axis=0)
                query = jnp.concatenate([part * low, part * high], axis=0).astype(BF16)
                q1[PER * j + r] = query
                keys = (PER * j + r, pl.ds(0, BLOCK))
                acc1[PER * j + r] = attend(query, [(k1[keys], v1[keys], mfar[:, :BLOCK])])

    def far_layer(chunks):
        attended = []
        far_keys([(j, d) for j in chunks for d in (1, 2)])
        for j in chunks:
            found = {}
            for r, rows in enumerate(residues(j)):
                keys = (PER * j + r, pl.ds(BLOCK, 2 * BLOCK))
                result = acc1[PER * j + r] + attend(
                    q1[PER * j + r], [(k1[keys], v1[keys], mfar[:, BLOCK:])]
                )
                result = result[:, :D] / result[:, D:]
                for t, i in enumerate(rows):
                    found[i] = result[t * COLS : (t + 1) * COLS]
            order = [t for _, rows in pieces_of(j) for seg in segments(rows) for t in seg]
            attended += [found[i][a:b] for i, a, b in order]
        x = jnp.concatenate([x2[j] for j in chunks], axis=0)
        x = finish(x, jnp.concatenate(attended, axis=0), 1)
        for at, j in enumerate(chunks):
            for i in ROWS_OF[j]:
                rows = whole_rows(x[at * TOK : (at + 1) * TOK], j, [i])
                out[i] = jnp.concatenate(rows, axis=0).astype(BF16)

    outer_columns()
    far_halo()
    edge_rows()
    last = range(1, CHUNKS)
    relay([0], 0)
    relay(last, 0)
    far_own([0])
    relay(last, 1)
    received(centres[0] + relays[0])
    far_layer([0])
    far_own(last)
    received(sum([centres[j] + relays[j] for j in last], []))
    far_layer(last)
    each(near_copies + sum(sides + centres + relays, []), lambda copy: copy.wait_send())


def shards(tokens, attn_gain, w_qkv, score_scale, w_out, mlp_gain, w_in, down_weight):
    operands = (tokens, attn_gain, w_qkv, score_scale, w_out, mlp_gain, w_in, down_weight)
    operands = [pltpu.with_memory_space_constraint(a, pltpu.HBM) for a in operands]
    return pl.pallas_call(
        kernel,
        out_shape=jax.ShapeDtypeStruct((ROWS, COLS, D), BF16),
        in_specs=[pl.BlockSpec(memory_space=pltpu.HBM)] * OPERANDS,
        out_specs=pl.BlockSpec(memory_space=pltpu.VMEM),
        scratch_shapes=[pltpu.VMEM(a.shape, a.dtype) for a in operands]
        + [
            pltpu.SemaphoreType.DMA((OPERANDS,)),
            pltpu.VMEM((64, 256), BF16),
            pltpu.VMEM((64, 64), BF16),
            pltpu.VMEM((128, 80), BF16),
            pltpu.VMEM((TRIPS * COLS, 3 * BLOCK), BF16),
            pltpu.VMEM((ROWS * COLS, D), BF16),
            pltpu.VMEM((ROWS * COLS, 2 * D), BF16),
            pltpu.VMEM((192, D), BF16),
            pltpu.VMEM((192, 2 * D), BF16),
            pltpu.VMEM((256, D), BF16),
            pltpu.VMEM((256, 2 * D), BF16),
            pltpu.VMEM((2, ROWS * COLS, D), BF16),
            pltpu.VMEM((ROWS * COLS, 2 * D), F32),
            pltpu.VMEM((CHUNKS, TOK, D), F32),
            pltpu.VMEM((3, COLS, D), BF16),
            pltpu.VMEM((3, COLS, D), BF16),
            pltpu.VMEM((96, D), BF16),
            pltpu.VMEM((96, D), BF16),
            pltpu.VMEM((2, 128, D), BF16),
            pltpu.VMEM((CHUNKS, TOK, D), BF16),
            pltpu.VMEM((2, CHUNKS, TOK, D), BF16),
            pltpu.VMEM((3, CHUNKS, 2, SIDE, D), BF16),
            pltpu.VMEM((STEP, 2 * TRIPS * COLS, D), BF16),
            pltpu.VMEM((STEP, 3 * BLOCK, D), BF16),
            pltpu.VMEM((STEP, 3 * BLOCK, 2 * D), BF16),
            pltpu.VMEM((STEP, TRIPS * COLS, 2 * D), F32),
            pltpu.SemaphoreType.DMA((6,)),
            pltpu.SemaphoreType.DMA((6,)),
            pltpu.SemaphoreType.DMA((CHUNKS, 14)),
            pltpu.SemaphoreType.DMA((CHUNKS, 14)),
        ],
        compiler_params=pltpu.CompilerParams(
            collective_id=0, has_side_effects=True, vmem_limit_bytes=48 * 1024 * 1024
        ),
        name="two_layers",
    )(*operands)


def solution(mesh):
    return jax.shard_map(
        shards,
        mesh=mesh,
        in_specs=(P("row", "col", None), P(), P(), P(), P(), P(), P(), P()),
        out_specs=P("row", "col", None),
        check_vma=False,
    )
```
